512 devices in a mesh: ctx: 8 (over z_hi, x), ep: 64 (over z_lo, y, core).
Axes of the slice: x: 4, y: 8, z: 8 (z_hi: 2, z_lo: 4; z = z_hi * 4 + z_lo), core: 2. Of those that a mesh axis runs over, the one named last changes fastest.
Arguments:
- moe_rows: bfloat16 [65536, 2048], P(('ctx', 'ep')), may hold values from -6 to 6
- expert_ids: int32 [65536, 8], P(('ctx', 'ep')), may hold values from 0 to 127, all different within a row; in each aligned block of 128 rows (0 to 127, 128 to 255, ...) at most 9 rows name the same one
- expert_gates: bfloat16 [65536, 8], P(('ctx', 'ep')), may hold values from 0.049804688 to 1
- expert_weights: bfloat16 [128, 2048, 1536], P('ep', 'ctx'), may hold values from -0.125 to 0.125
Outputs:
- expert_hidden: bfloat16 [8, 128, 64, 9, 768], P('ctx', 'ep')
The draws below stay inside these ranges and needn't reach their ends.
Inputs may be any that keep to these rules, and one draw needn't show every extreme that they name: `expert_ids`: each token names 8 different experts; in each aligned block of 128 tokens (the tokens of one device) no expert is named more than 9 times, a bound that some block reaches.
All inputs are finite; a program needn't handle non-finite values.
Results may differ from the reference program's by a relative error of at most 0.0012.
Values may be sent and summed in bfloat16 or wider, within the bound.
No kernel may reach another device: no remote copies, remote signals or barrier semaphores. Data moves between devices by JAX's collectives and lax.ppermute only.
A program may use at most 128 MiB of HBM per device.

```python
import math
import jax
import jax.numpy as jnp
import numpy as np
from jax import lax

D = 2048
FF = 768
TOP = 8
TOK_DEV = 128
TOKENS = 65536
EXPERTS = 128
CAP = 9
N_CTX = 8
N_EP = 64


def block_scale(stream_key, dims, cuts, least, high):
    loudness = 1.0
    for dim, blocks in cuts:
        heights = jax.random.uniform(jax.random.fold_in(jax.random.fold_in(stream_key, 6), dim), (blocks,), jnp.float32, least / len(cuts), high / len(cuts))
        loudness = loudness * jnp.repeat(jnp.exp(heights), dims[dim] // blocks).reshape((-1,) + (1,) * (len(dims) - 1 - dim))
    return loudness


def shared_out(rng, own, number, rows, count, top, limit, skew):
    order = jax.random.permutation(rng, count)
    packed, ordinary = load_shares(count, rows * top, limit, skew, True), load_shares(count, rows * top, limit, skew, False)
    places = jnp.arange(count)

    def named(sizes, rotation):
        used = int((sizes > 0).sum())
        fixed = max(1, used // 4)
        passed = fixed + (places - fixed + rotation * (used - fixed)) % max(1, count - fixed)
        return jnp.zeros((count,), jnp.int32).at[order[jnp.where(places < fixed, places, passed)]].set(jnp.asarray(sizes, jnp.int32))

    sizes = jnp.where(number % 4 == 0, named(packed, number // 4), named(ordinary, number - number // 4 - 1))
    mixed = jax.random.permutation(jax.random.fold_in(own, 3), count)
    giver, sink = mixed[0:count // 2 * 2:2], mixed[1:count // 2 * 2:2]
    room = jnp.minimum(sizes[giver] - 1, limit - sizes[sink]) // 2
    room = jnp.where((giver == order[0]) | (sink == order[0]) | (sizes[sink] == 0), 0, jnp.maximum(room, 0))
    passed = jax.random.randint(jax.random.fold_in(own, 4), (count // 2,), 0, 1 << 20) % (room + 1)
    sizes = sizes.at[giver].add(-passed).at[sink].add(passed)
    members = jnp.searchsorted(jnp.cumsum(sizes), jnp.arange(rows * top), side="right").astype(jnp.int32)
    table = members.reshape(top, rows).T
    table = table[jax.random.permutation(jax.random.fold_in(own, 1), rows)]
    rotation = jax.random.randint(jax.random.fold_in(own, 2), (rows, 1), 0, top)
    return jnp.take_along_axis(table, (jnp.arange(top)[None, :] + rotation) % top, axis=1)


def load_shares(count, total, reach, skew, full):
    weights = [(1 << 20) // math.isqrt(grade ** skew) + 1 for grade in range(1, count + 1)]
    largest = reach if full else min(reach, max(-(-total // count), total * weights[0] // sum(weights)))
    least = 1 if total - largest >= count - 1 else 0
    given, surplus = [largest] + [least] * (count - 1), total - largest - least * (count - 1)
    while surplus > 0:
        movable = [i for i in range(1, count) if given[i] < largest] or [i for i in range(1, count) if given[i] < reach]
        whole, remaining = sum([weights[i] for i in movable]), surplus
        for i in movable:
            extra = min(reach - given[i], max(1, remaining * weights[i] // whole), surplus)
            given[i] = given[i] + extra
            surplus = surplus - extra
    return np.array(given)


def scatter_about(own_key, extent, deviation, bound, cuts=(), held_as=jnp.bfloat16):
    values = deviation * jax.random.normal(own_key, extent, jnp.float32)
    if cuts:
        values = values * block_scale(own_key, extent, cuts, -0.22, 0.18)
    return jnp.clip(values, -bound, bound).astype(held_as)


def setup_inputs(seed: int = 0) -> dict:
    key_list = jax.random.split(jax.random.key(seed), 5)
    moe_rows = scatter_about(key_list[0], (TOKENS, D), 1.0, 6.0, ((0, 512),))
    expert_ids_keys = jax.random.split(jax.random.fold_in(key_list[1], 1), TOKENS // TOK_DEV)
    expert_ids_turns = jax.random.permutation(jax.random.fold_in(key_list[1], 3), TOKENS // TOK_DEV)
    expert_ids = jax.vmap(lambda own, number: shared_out(jax.random.fold_in(key_list[1], 2), own, number, TOK_DEV, EXPERTS, TOP, CAP, 2))(expert_ids_keys, expert_ids_turns).reshape((TOKENS, TOP))
    expert_gates = jnp.clip(0.049804688 + 0.9501953 * jax.random.uniform(key_list[2], (TOKENS, TOP), jnp.float32) ** block_scale(key_list[2], (TOKENS, TOP), ((0, 512),), -0.2, 0.2), 0.049804688, 1.0).astype(jnp.bfloat16)
    expert_weights = scatter_about(key_list[3], (EXPERTS, D, 2 * FF), D ** -0.5, 0.125, ((0, 64), (1, 8)))
    return dict(moe_rows=moe_rows, expert_ids=expert_ids, expert_gates=expert_gates, expert_weights=expert_weights)


def place_rows(block_rows, block_ids, block_gates, experts, capacity):
    flat_ids = block_ids.reshape(-1).astype(jnp.int32)
    markers = (flat_ids[:, None] == jnp.arange(experts, dtype=jnp.int32)[None, :]).astype(jnp.int32)
    ranking = (jnp.cumsum(markers, axis=0) - markers).astype(jnp.int32)
    slot_index = jnp.sum(ranking * markers, axis=1).astype(jnp.int32)
    places = (flat_ids * capacity + slot_index).astype(jnp.int32)
    owners = (jnp.arange(flat_ids.shape[0], dtype=jnp.int32) // block_ids.shape[1]).astype(jnp.int32)
    buffer = jnp.zeros((experts * capacity, block_rows.shape[1]), block_rows.dtype).at[places].set(block_rows[owners])
    gate_buffer = jnp.zeros((experts * capacity,), block_gates.dtype).at[places].set(block_gates.reshape(-1))
    return buffer.reshape(experts, capacity, block_rows.shape[1]), gate_buffer.reshape(experts, capacity)


def place_block(block_rows, block_ids, block_gates):
    return place_rows(block_rows, block_ids, block_gates, EXPERTS, CAP)


def reference(moe_rows, expert_ids, expert_gates, expert_weights):
    block_rows = moe_rows.reshape(N_CTX, N_EP, TOK_DEV, D)
    block_ids = expert_ids.reshape(N_CTX, N_EP, TOK_DEV, TOP)
    block_gates = expert_gates.reshape(N_CTX, N_EP, TOK_DEV, TOP)

    def per_block(block_index):
        buffers, gate_buffers = jax.vmap(place_block)(block_rows[block_index], block_ids[block_index], block_gates[block_index])

        def per_expert(expert_index):
            gathered = buffers[:, expert_index].reshape(N_EP * CAP, D)
            before = jnp.dot(gathered, expert_weights[expert_index], preferred_element_type=jnp.float32)
            scaled = gate_buffers[:, expert_index].reshape(N_EP * CAP, 1).astype(jnp.float32)
            hidden = jax.nn.silu(before[:, :FF]) * before[:, FF:] * scaled
            return hidden.astype(jnp.bfloat16).reshape(N_EP, CAP, FF)

        return lax.map(per_expert, jnp.arange(EXPERTS, dtype=jnp.int32))

    return lax.map(per_block, jnp.arange(N_CTX, dtype=jnp.int32))
```

```python
import jax
import jax.numpy as jnp
from jax import lax
from jax.experimental import pallas as pl
from jax.experimental.pallas import tpu as pltpu
from jax.sharding import Mesh, PartitionSpec as P

ZH, X, ZL, Y, C = 2, 4, 4, 8, 2
PEERS = Y * C
HELD = 2
CAP = 9
MAIN = CAP - 1
TOP = 8
TOK = 128
D = 2048
FF = 768
KEPT = PEERS * HELD
REST = (ZL - 1) * MAIN
MSG = HELD * CAP * ZL
TAIL = MSG - HELD * ZL
COLS = 512
TILE = 256
INFO = 2 * TOK

f32 = jnp.float32
bf16 = jnp.bfloat16


def iota(shape, dim):
    return lax.broadcasted_iota(jnp.int32, shape, dim)


def earlier():
    return (iota((TOK, TOK), 0) < iota((TOK, TOK), 1)).astype(bf16)


def named(ids, experts):
    hit = (ids[0:1, :] == experts).astype(f32)
    for k in range(1, TOP):
        hit = hit + (ids[k : k + 1, :] == experts).astype(f32)
    return hit


def dispatch_kernel(zl_ref, *refs):
    blocks, out_ref, main_ref, tail_ref = refs[:ZL], refs[ZL], refs[ZL + 1], refs[ZL + 2]

    @pl.when(pl.program_id(0) == 0)
    def _():
        first = zl_ref[0] * KEPT
        before = earlier()
        kept = (iota((KEPT, TOK), 0) + first).astype(f32)
        row = iota((PEERS * ZL * HELD, TOK), 0)
        ending = (first + row // (ZL * HELD) * HELD + row % HELD).astype(f32)
        for b in range(ZL):
            ids = blocks[b][TOK : TOK + TOP, 0:TOK].astype(f32)
            hit = named(ids, kept)
            rank = jnp.dot(hit.astype(bf16), before, preferred_element_type=f32)
            place = jnp.where(hit > 0, rank, -1.0)
            slot = iota((KEPT, MAIN, TOK), 1).astype(f32)
            chosen = (place[:, None, :] == slot).astype(f32)
            main_ref[b] = chosen.reshape(KEPT * MAIN, TOK).astype(bf16)
            hit = jnp.where(row // HELD % ZL == b, named(ids, ending), 0.0)
            rank = jnp.dot(hit.astype(bf16), before, preferred_element_type=f32)
            chosen = jnp.where(rank == MAIN, hit, 0.0)
            tail_ref[b] = chosen.astype(bf16)

    width = out_ref.shape[2]
    last = jnp.zeros((PEERS * ZL * HELD, width), f32)
    for b in range(ZL):
        rows = blocks[b][0:TOK, :]
        moved = jnp.dot(main_ref[b], rows, preferred_element_type=f32).astype(bf16)
        moved = moved.reshape(PEERS, HELD, MAIN, width)
        for e in range(HELD):
            at = e * MAIN if b == 0 else HELD * MAIN + e * REST + (b - 1) * MAIN
            out_ref[:, at : at + MAIN, :] = moved[:, e]
        last = last + jnp.dot(tail_ref[b], rows, preferred_element_type=f32)
    out_ref[:, TAIL:MSG, :] = last.astype(bf16).reshape(PEERS, ZL * HELD, width)


def dispatch(zl, blocks):
    return pl.pallas_call(
        dispatch_kernel,
        grid_spec=pltpu.PrefetchScalarGridSpec(
            num_scalar_prefetch=1,
            grid=(D // COLS,),
            in_specs=[pl.BlockSpec((TOK + TOP, COLS), lambda n, z: (0, n))] * ZL,
            out_specs=pl.BlockSpec((PEERS, MSG, COLS), lambda n, z: (0, 0, n)),
            scratch_shapes=[
                pltpu.VMEM((ZL, KEPT * MAIN, TOK), bf16),
                pltpu.VMEM((ZL, PEERS * ZL * HELD, TOK), bf16),
            ],
        ),
        out_shape=jax.ShapeDtypeStruct((PEERS, MSG, D), bf16),
        compiler_params=pltpu.CompilerParams(vmem_limit_bytes=40 * 1024 * 1024),
        cost_estimate=pl.CostEstimate(
            flops=2 * ZL * 384 * TOK * D, bytes_accessed=7_000_000, transcendentals=0
        ),
    )(zl, *blocks)


def expert_kernel(
    where_ref, x_ref, info_ref, g0_ref, g1_ref, u0_ref, u1_ref, out_ref,
    rows_ref, gate_ref, sort_ref, sort8_ref,
):
    blocks = PEERS * ZL
    count = blocks * MAIN
    zl, zh, first = where_ref[0], where_ref[1], where_ref[2]
    e, n = pl.program_id(0), pl.program_id(1)

    @pl.when((e == 0) & (n == 0))
    def _():
        out_row, in_row = iota((count, count), 0), iota((count, count), 1)
        late = in_row - PEERS * MAIN
        is_late = late >= 0
        peer = jnp.where(is_late, late // REST, in_row // MAIN)
        b = jnp.where(is_late, late % REST // MAIN + 1, 0)
        slot = in_row % MAIN
        source = (zl - b + ZL) % ZL * PEERS + peer
        sort_ref[...] = (out_row == slot * blocks + source).astype(f32).astype(bf16)

    @pl.when(n == 0)
    def _():
        near = pl.ds(pl.multiple_of(zh * (D // 2), D // 2), D // 2)
        far = pl.ds(pl.multiple_of((1 - zh) * (D // 2), D // 2), D // 2)
        for half, cols in enumerate((near, far)):
            to = slice(half * (D // 2), (half + 1) * (D // 2))
            for mine in range(HELD):

                @pl.when(e == mine)
                def _():
                    at = mine * MAIN
                    rows_ref[0 : PEERS * MAIN, to] = x_ref[:, at : at + MAIN, cols].reshape(
                        PEERS * MAIN, D // 2
                    )
                    at = HELD * MAIN + mine * REST
                    rows_ref[PEERS * MAIN : count, to] = x_ref[:, at : at + REST, cols].reshape(
                        PEERS * REST, D // 2
                    )

            rows_ref[count:, to] = x_ref[:, TAIL:MSG, cols].reshape(blocks * HELD, D // 2)

        expert = (first + e).astype(f32)
        hit = jnp.zeros((blocks, TOK), f32)
        gate = jnp.zeros((blocks, TOK), f32)
        for k in range(TOP):
            same = info_ref[k, :, 0:TOK].astype(f32) == expert
            hit = hit + same.astype(f32)
            gate = gate + jnp.where(same, info_ref[k, :, TOK:INFO].astype(f32), 0.0)
        rank = jnp.dot(hit.astype(bf16), earlier(), preferred_element_type=f32)
        ones = jnp.ones((TOK, TILE), bf16)
        slot = iota((blocks, MAIN, TOK), 1).astype(f32)
        chosen = jnp.where(rank[:, None, :] == slot, gate[:, None, :], 0.0)
        near_rows = PEERS * MAIN
        chosen = chosen.reshape(ZL, near_rows, TOK)
        gate_ref[0:near_rows, :] = jnp.dot(
            chosen[0].astype(bf16), ones, preferred_element_type=f32
        )
        others = jnp.concatenate(
            [chosen[b].reshape(PEERS, MAIN, TOK) for b in range(1, ZL)], axis=1
        ).reshape(PEERS * REST, TOK)
        gate_ref[near_rows:count, :] = jnp.dot(
            others.astype(bf16), ones, preferred_element_type=f32
        )
        last = jnp.where(rank == MAIN, gate, 0.0).astype(bf16)
        last = jnp.dot(last, ones, preferred_element_type=f32).astype(bf16)
        row, col = iota((blocks * HELD, blocks), 0), iota((blocks * HELD, blocks), 1)
        peer, b = row // (ZL * HELD), row // HELD % ZL
        spread = (col == b * PEERS + peer).astype(f32).astype(bf16)
        gate_ref[count:, :] = jnp.dot(spread, last, preferred_element_type=f32)
        out_row, in_row = iota((blocks, blocks * HELD), 0), iota((blocks, blocks * HELD), 1)
        peer, b = in_row // (ZL * HELD), in_row // HELD % ZL
        source = (zl - b + ZL) % ZL * PEERS + peer
        keep = (out_row == source) & (in_row % HELD == e)
        sort8_ref[...] = keep.astype(f32).astype(bf16)

    half = D // 2
    left, right = rows_ref[:, 0:half], rows_ref[:, half:]

    def times(near_ref, far_ref):
        return jnp.dot(
            left, near_ref[...].reshape(half, TILE), preferred_element_type=f32
        ) + jnp.dot(right, far_ref[...].reshape(half, TILE), preferred_element_type=f32)

    before = times(g0_ref, g1_ref)
    up = times(u0_ref, u1_ref)
    hidden = (before / (1.0 + jnp.exp(-before)) * up * gate_ref[...]).astype(bf16)
    main = jnp.dot(sort_ref[...], hidden[0:count], preferred_element_type=f32)
    out_ref[0, 0:MAIN] = main.astype(bf16).reshape(MAIN, blocks, TILE)
    last = jnp.dot(sort8_ref[...], hidden[count:], preferred_element_type=f32)
    out_ref[0, MAIN] = last.astype(bf16)


def experts(where, arrived, info, near, far):
    blocks = PEERS * ZL
    tiles = FF // TILE
    rows = blocks * (MAIN + HELD)
    gate = pl.BlockSpec((X, 1, D // 8, TILE), lambda e, n, w: (0, e, 0, n))
    up = pl.BlockSpec((X, 1, D // 8, TILE), lambda e, n, w: (0, e, 0, n + tiles))
    return pl.pallas_call(
        expert_kernel,
        grid_spec=pltpu.PrefetchScalarGridSpec(
            num_scalar_prefetch=1,
            grid=(HELD, tiles),
            in_specs=[
                pl.BlockSpec((PEERS, MSG, D), lambda e, n, w: (0, 0, 0)),
                pl.BlockSpec((TOP, blocks, INFO), lambda e, n, w: (0, 0, 0)),
                gate, gate, up, up,
            ],
            out_specs=pl.BlockSpec((1, CAP, blocks, TILE), lambda e, n, w: (e, 0, 0, n)),
            scratch_shapes=[
                pltpu.VMEM((rows, D), bf16),
                pltpu.VMEM((rows, TILE), f32),
                pltpu.VMEM((blocks * MAIN, blocks * MAIN), bf16),
                pltpu.VMEM((blocks, blocks * HELD), bf16),
            ],
        ),
        out_shape=jax.ShapeDtypeStruct((HELD, CAP, blocks, FF), bf16),
        compiler_params=pltpu.CompilerParams(vmem_limit_bytes=48 * 1024 * 1024),
        cost_estimate=pl.CostEstimate(
            flops=2 * HELD * rows * D * 2 * FF, bytes_accessed=20_000_000, transcendentals=10**6
        ),
    )(where, arrived, info, near, far, near, far)


def shards(moe_rows, expert_ids, expert_gates, expert_weights):
    zh, zl = lax.axis_index("zh"), lax.axis_index("zl")
    peer = lax.axis_index(("y", "c"))
    info = jnp.concatenate([expert_ids.T.astype(bf16), expert_gates.T], axis=1)
    packed = jnp.concatenate([moe_rows, jnp.pad(info, ((0, 0), (0, D - INFO)))], axis=0)
    blocks = [packed] + [
        lax.ppermute(packed, "zl", [(i, (i + b) % ZL) for i in range(ZL)]) for b in range(1, ZL)
    ]
    near = lax.all_gather(expert_weights, "x", axis=0)
    swapped = lax.ppermute(expert_weights, "zh", [(0, 1), (1, 0)])
    far = lax.all_gather(swapped, "x", axis=0)
    message = dispatch(zl.reshape(1), blocks)
    arrived = lax.all_to_all(message, ("y", "c"), split_axis=0, concat_axis=0, tiled=True)
    known = jnp.stack([block[TOK:, 0:INFO] for block in blocks], axis=1)
    known = lax.all_gather(known, ("y", "c"), axis=0)
    known = jnp.transpose(known, (1, 2, 0, 3)).reshape(TOP, ZL * PEERS, INFO)
    where = jnp.stack([zl, zh, (zl * PEERS + peer) * HELD])
    hidden = experts(where, arrived, known, near, far)
    return jnp.transpose(hidden, (0, 2, 1, 3))[None]


def solution(mesh):
    inner = Mesh(mesh.devices.reshape(ZH, X, ZL, Y, C), ("zh", "x", "zl", "y", "c"))
    tokens = P(("zh", "x", "zl", "y", "c"), None)
    in_specs = (tokens, tokens, tokens, P(("zl", "y", "c"), ("zh", "x"), None))
    out_specs = P(("zh", "x"), ("zl", "y", "c"), None, None, None)
    return jax.shard_map(
        shards, mesh=inner, in_specs=in_specs, out_specs=out_specs, check_vma=False
    )
```

```python
import jax
import jax.numpy as jnp
from jax import lax
from jax.experimental import pallas as pl
from jax.experimental.pallas import tpu as pltpu
from jax.sharding import Mesh, PartitionSpec as P

ZH, X, ZL, Y, C = 2, 4, 4, 8, 2
PEERS = Y * C
HELD = 2
CAP = 9
MAIN = CAP - 1
TOP = 8
TOK = 128
D = 2048
FF = 768
KEPT = PEERS * HELD
LEFT = (ZL - 1) * HELD
COLS = 512
TILE = 256
INFO = 2 * TOK

f32 = jnp.float32
bf16 = jnp.bfloat16


def iota(shape, dim):
    return lax.broadcasted_iota(jnp.int32, shape, dim)


def earlier():
    return (iota((TOK, TOK), 0) < iota((TOK, TOK), 1)).astype(bf16)


def named(ids, experts):
    hit = (ids[0:1, :] == experts).astype(f32)
    for k in range(1, TOP):
        hit = hit + (ids[k : k + 1, :] == experts).astype(f32)
    return hit


def chosen_rows(ids, first):
    kept = (iota((KEPT, TOK), 0) + first).astype(f32)
    hit = named(ids, kept)
    rank = jnp.dot(hit.astype(bf16), earlier(), preferred_element_type=f32)
    place = jnp.where(hit > 0, rank, -1.0)
    slot = iota((KEPT, MAIN, TOK), 1).astype(f32)
    chosen = (place[:, None, :] == slot).astype(f32)
    return chosen.reshape(KEPT * MAIN, TOK).astype(bf16)


def moved_rows(chosen, rows):
    moved = jnp.dot(chosen, rows, preferred_element_type=f32).astype(bf16)
    return moved.reshape(PEERS, HELD, MAIN, rows.shape[1])


def ids_of(block):
    return block[TOK : TOK + TOP, 0:TOK].astype(f32)


def own_kernel(zl_ref, block, out_ref, main_ref):
    @pl.when(pl.program_id(0) == 0)
    def _():
        main_ref[...] = chosen_rows(ids_of(block), zl_ref[0] * KEPT)

    out_ref[:, 0:HELD] = moved_rows(main_ref[...], block[0:TOK, :])
    info = block[TOK : TOK + TOP, :]
    out_ref[:, HELD] = jnp.broadcast_to(info[None], (PEERS,) + info.shape)


def rest_kernel(zl_ref, *refs):
    blocks, out_ref, main_ref, tail_ref = refs[:ZL], refs[ZL], refs[ZL + 1], refs[ZL + 2]

    @pl.when(pl.program_id(0) == 0)
    def _():
        first = zl_ref[0] * KEPT
        row = iota((PEERS * ZL * HELD, TOK), 0)
        ending = (first + row // (ZL * HELD) * HELD + row % HELD).astype(f32)
        for b in range(ZL):
            ids = ids_of(blocks[b])
            if b:
                main_ref[b - 1] = chosen_rows(ids, first)
            hit = jnp.where(row // HELD % ZL == b, named(ids, ending), 0.0)
            rank = jnp.dot(hit.astype(bf16), earlier(), preferred_element_type=f32)
            tail_ref[b] = jnp.where(rank == MAIN, hit, 0.0).astype(bf16)

    width = out_ref.shape[3]
    last = jnp.zeros((PEERS * ZL * HELD, width), f32)
    for b in range(ZL):
        rows = blocks[b][0:TOK, :]
        if b:
            moved = moved_rows(main_ref[b - 1], rows)
            for e in range(HELD):
                out_ref[:, e * (ZL - 1) + b - 1] = moved[:, e]
        last = last + jnp.dot(tail_ref[b], rows, preferred_element_type=f32)
    out_ref[:, LEFT] = last.astype(bf16).reshape(PEERS, ZL * HELD, width)


def dispatch(kernel, tiles, scratch, zl, blocks):
    return pl.pallas_call(
        kernel,
        grid_spec=pltpu.PrefetchScalarGridSpec(
            num_scalar_prefetch=1,
            grid=(D // COLS,),
            in_specs=[pl.BlockSpec((TOK + TOP, COLS), lambda n, z: (0, n))] * len(blocks),
            out_specs=pl.BlockSpec((PEERS, tiles, MAIN, COLS), lambda n, z: (0, 0, 0, n)),
            scratch_shapes=scratch,
        ),
        out_shape=jax.ShapeDtypeStruct((PEERS, tiles, MAIN, D), bf16),
        compiler_params=pltpu.CompilerParams(vmem_limit_bytes=40 * 1024 * 1024),
        cost_estimate=pl.CostEstimate(
            flops=2 * len(blocks) * 384 * TOK * D,
            bytes_accessed=PEERS * tiles * MAIN * D * 2,
            transcendentals=0,
        ),
    )(zl, *blocks)


def plan_kernel(where_ref, info_ref, gate_ref, sort_ref, sort8_ref):
    blocks = PEERS * ZL
    count = blocks * MAIN
    near_rows = PEERS * MAIN
    rest = (ZL - 1) * MAIN
    zl, first = where_ref[0], where_ref[2]
    out_row, in_row = iota((count, count), 0), iota((count, count), 1)
    late = in_row - near_rows
    peer = jnp.where(late >= 0, late // rest, in_row // MAIN)
    b = jnp.where(late >= 0, late % rest // MAIN + 1, 0)
    source = (zl - b + ZL) % ZL * PEERS + peer
    sort_ref[...] = (out_row == in_row % MAIN * blocks + source).astype(f32).astype(bf16)
    ones = jnp.ones((TOK, TILE), bf16)
    for e in range(HELD):
        expert = (first + e).astype(f32)
        hit = jnp.zeros((blocks, TOK), f32)
        gate = jnp.zeros((blocks, TOK), f32)
        for k in range(TOP):
            same = info_ref[k, :, 0:TOK].astype(f32) == expert
            hit = hit + same.astype(f32)
            gate = gate + jnp.where(same, info_ref[k, :, TOK:INFO].astype(f32), 0.0)
        rank = jnp.dot(hit.astype(bf16), earlier(), preferred_element_type=f32)
        slot = iota((blocks, MAIN, TOK), 1).astype(f32)
        chosen = jnp.where(rank[:, None, :] == slot, gate[:, None, :], 0.0)
        chosen = chosen.reshape(ZL, near_rows, TOK)
        gate_ref[e, 0:near_rows, :] = jnp.dot(
            chosen[0].astype(bf16), ones, preferred_element_type=f32
        )
        others = jnp.concatenate(
            [chosen[b].reshape(PEERS, MAIN, TOK) for b in range(1, ZL)], axis=1
        ).reshape(PEERS * rest, TOK)
        gate_ref[e, near_rows:count, :] = jnp.dot(
            others.astype(bf16), ones, preferred_element_type=f32
        )
        last = jnp.where(rank == MAIN, gate, 0.0).astype(bf16)
        last = jnp.dot(last, ones, preferred_element_type=f32).astype(bf16)
        row, col = iota((blocks * HELD, blocks), 0), iota((blocks * HELD, blocks), 1)
        spread = (col == row // HELD % ZL * PEERS + row // (ZL * HELD)).astype(f32).astype(bf16)
        gate_ref[e, count:, :] = jnp.dot(spread, last, preferred_element_type=f32)
        out_row, in_row = iota((blocks, blocks * HELD), 0), iota((blocks, blocks * HELD), 1)
        source = (zl - in_row // HELD % ZL + ZL) % ZL * PEERS + in_row // (ZL * HELD)
        keep = (out_row == source) & (in_row % HELD == e)
        sort8_ref[e] = keep.astype(f32).astype(bf16)


def plan(where, info):
    blocks = PEERS * ZL
    rows = blocks * (MAIN + HELD)
    shapes = [
        jax.ShapeDtypeStruct((HELD, rows, TILE), f32),
        jax.ShapeDtypeStruct((blocks * MAIN, blocks * MAIN), bf16),
        jax.ShapeDtypeStruct((HELD, blocks, blocks * HELD), bf16),
    ]
    return pl.pallas_call(
        plan_kernel,
        grid_spec=pltpu.PrefetchScalarGridSpec(
            num_scalar_prefetch=1,
            grid=(1,),
            in_specs=[pl.BlockSpec(info.shape, lambda n, w: (0, 0, 0))],
            out_specs=[
                pl.BlockSpec(s.shape, lambda n, w, r=len(s.shape): (0,) * r) for s in shapes
            ],
        ),
        out_shape=shapes,
        compiler_params=pltpu.CompilerParams(vmem_limit_bytes=32 * 1024 * 1024),
        cost_estimate=pl.CostEstimate(flops=10**8, bytes_accessed=10**6, transcendentals=0),
    )(where, info)


def gather_rows(rows_ref, own_ref, rest_ref, last_ref):
    at = 0
    for ref in (own_ref, rest_ref, last_ref):
        count = ref.shape[0] * ref.shape[1] * ref.shape[2]
        rows_ref[at : at + count, :] = ref[...].reshape(count, ref.shape[3])
        at += count


def near_kernel(where_ref, own_ref, rest_ref, last_ref, weights_ref, out_ref, rows_ref):
    @pl.when(pl.program_id(1) == 0)
    def _():
        gather_rows(rows_ref, own_ref, rest_ref, last_ref)

    weights = weights_ref[...].reshape(D // 2, weights_ref.shape[3])
    out_ref[0] = jnp.dot(rows_ref[...], weights, preferred_element_type=f32)


def near_part(where, own, rest, near):
    rows, half, tile = PEERS * ZL * (MAIN + HELD), D // 2, 2 * TILE
    return pl.pallas_call(
        near_kernel,
        grid_spec=pltpu.PrefetchScalarGridSpec(
            num_scalar_prefetch=1,
            grid=(HELD, 2 * FF // tile),
            in_specs=[
                pl.BlockSpec((PEERS, 1, MAIN, half), lambda e, n, w: (0, e, 0, w[1])),
                pl.BlockSpec((PEERS, ZL - 1, MAIN, half), lambda e, n, w: (0, e, 0, w[1])),
                pl.BlockSpec((PEERS, 1, MAIN, half), lambda e, n, w: (0, LEFT, 0, w[1])),
                pl.BlockSpec((X, 1, D // 8, tile), lambda e, n, w: (0, e, 0, n)),
            ],
            out_specs=pl.BlockSpec((1, rows, tile), lambda e, n, w: (e, 0, n)),
            scratch_shapes=[pltpu.VMEM((rows, half), bf16)],
        ),
        out_shape=jax.ShapeDtypeStruct((HELD, rows, 2 * FF), f32),
        compiler_params=pltpu.CompilerParams(vmem_limit_bytes=40 * 1024 * 1024),
        cost_estimate=pl.CostEstimate(flops=10**11, bytes_accessed=10**7, transcendentals=0),
    )(where, own, rest, rest, near)


def expert_kernel(
    where_ref, own_ref, rest_ref, last_ref, gate_ref, sort_ref, sort8_ref,
    before_ref, up_ref, g_ref, u_ref, *refs,
):
    out_ref, rows_ref = refs[-2:]
    blocks = PEERS * ZL
    count = blocks * MAIN
    half = D // 2

    @pl.when(pl.program_id(0) == 0)
    def _():
        gather_rows(rows_ref, own_ref, rest_ref, last_ref)

    def added(sums_ref, weights_ref):
        weights = weights_ref[...].reshape(half, TILE)
        return sums_ref[0] + jnp.dot(rows_ref[...], weights, preferred_element_type=f32)

    before = added(before_ref, g_ref)
    up = added(up_ref, u_ref)
    hidden = (before / (1.0 + jnp.exp(-before)) * up * gate_ref[0]).astype(bf16)
    main = jnp.dot(sort_ref[...], hidden[0:count], preferred_element_type=f32)
    out_ref[0, 0:MAIN] = main.astype(bf16).reshape(MAIN, blocks, TILE)
    last = jnp.dot(sort8_ref[0], hidden[count:], preferred_element_type=f32)
    out_ref[0, MAIN] = last.astype(bf16)


def expert(e, where, own, rest, slots, sums, far, other=None):
    blocks = PEERS * ZL
    tiles = FF // TILE
    rows, half = blocks * (MAIN + HELD), D // 2
    gates, sort, sort8 = slots
    others = [] if other is None else [other]
    return pl.pallas_call(
        expert_kernel,
        grid_spec=pltpu.PrefetchScalarGridSpec(
            num_scalar_prefetch=1,
            grid=(tiles,),
            in_specs=[
                pl.BlockSpec((PEERS, 1, MAIN, half), lambda n, w: (0, e, 0, 1 - w[1])),
                pl.BlockSpec((PEERS, ZL - 1, MAIN, half), lambda n, w: (0, e, 0, 1 - w[1])),
                pl.BlockSpec((PEERS, 1, MAIN, half), lambda n, w: (0, LEFT, 0, 1 - w[1])),
                pl.BlockSpec((1, rows, TILE), lambda n, w: (e, 0, 0)),
                pl.BlockSpec(sort.shape, lambda n, w: (0, 0)),
                pl.BlockSpec((1,) + sort8.shape[1:], lambda n, w: (e, 0, 0)),
                pl.BlockSpec((1, rows, TILE), lambda n, w: (e, 0, n)),
                pl.BlockSpec((1, rows, TILE), lambda n, w: (e, 0, n + tiles)),
                pl.BlockSpec((X, D // 8, TILE), lambda n, w: (0, 0, n)),
                pl.BlockSpec((X, D // 8, TILE), lambda n, w: (0, 0, n + tiles)),
            ]
            + [pl.BlockSpec(memory_space=pl.ANY)] * len(others),
            out_specs=pl.BlockSpec((1, CAP, blocks, TILE), lambda n, w: (e, 0, 0, n)),
            scratch_shapes=[pltpu.VMEM((rows, half), bf16)],
        ),
        out_shape=jax.ShapeDtypeStruct((HELD, CAP, blocks, FF), bf16),
        input_output_aliases={11: 0} if others else {},
        compiler_params=pltpu.CompilerParams(vmem_limit_bytes=40 * 1024 * 1024),
        cost_estimate=pl.CostEstimate(
            flops=rows * D * 2 * FF, bytes_accessed=10_000_000, transcendentals=10**6
        ),
    )(where, own, rest, rest, gates, sort, sort8, sums, sums, far, far, *others)


def over_zl(block):
    return [block] + [
        lax.ppermute(block, "zl", [(i, (i + b) % ZL) for i in range(ZL)]) for b in range(1, ZL)
    ]


def over_peers(message):
    return lax.all_to_all(message, ("y", "c"), split_axis=0, concat_axis=0, tiled=True)


def take_kernel(*refs):
    refs[-1][...] = refs[0][0]


def marks(*values):
    return [
        lax.slice(v, (0,) * v.ndim, (1,) * (v.ndim - 2) + (8, TOK)).reshape(8, TOK) for v in values
    ]


def take(weights, e, *others):
    shape = weights.shape[1:]
    others = marks(*others)
    return pl.pallas_call(
        take_kernel,
        grid=(1,),
        in_specs=[pl.BlockSpec((1,) + shape, lambda n: (e, 0, 0))]
        + [pl.BlockSpec(memory_space=pl.ANY)] * len(others),
        out_specs=pl.BlockSpec(shape, lambda n: (0, 0)),
        out_shape=jax.ShapeDtypeStruct(shape, weights.dtype),
        cost_estimate=pl.CostEstimate(flops=0, bytes_accessed=1_600_000, transcendentals=0),
    )(weights, *others)


def pass_kernel(*refs):
    pass


def after(value, *others):
    others = marks(*others)
    return pl.pallas_call(
        pass_kernel,
        in_specs=[pl.BlockSpec(memory_space=pl.ANY)] * (1 + len(others)),
        out_specs=pl.BlockSpec(memory_space=pl.ANY),
        out_shape=jax.ShapeDtypeStruct(value.shape, value.dtype),
        input_output_aliases={0: 0},
    )(value, *others)


def shards(moe_rows, expert_ids, expert_gates, expert_weights):
    zh, zl = lax.axis_index("zh"), lax.axis_index("zl")
    peer = lax.axis_index(("y", "c"))
    where = jnp.stack([zl, zh, (zl * PEERS + peer) * HELD])
    info = jnp.concatenate([expert_ids.T.astype(bf16), expert_gates.T], axis=1)
    packed = jnp.concatenate([moe_rows, jnp.pad(info, ((0, 0), (0, D - INFO)))], axis=0)
    near = lax.all_gather(expert_weights, "x", axis=0)
    blocks = over_zl(packed)
    picked = pltpu.VMEM((KEPT * MAIN, TOK), bf16)
    own = over_peers(dispatch(own_kernel, HELD + 1, [picked], zl.reshape(1), [packed]))
    scratch = [
        pltpu.VMEM((ZL - 1, KEPT * MAIN, TOK), bf16),
        pltpu.VMEM((ZL, PEERS * ZL * HELD, TOK), bf16),
    ]
    message = dispatch(rest_kernel, LEFT + 1, scratch, zl.reshape(1), blocks)
    rest = over_peers(message)
    swap = [(0, 1), (1, 0)]
    first = lax.ppermute(take(expert_weights, 0, own, message), "zh", swap)
    second = lax.ppermute(take(expert_weights, 1, first), "zh", swap)
    far = [lax.all_gather(after(first, near), "x", axis=0), lax.all_gather(second, "x", axis=0)]
    known = jnp.stack(over_zl(own[:, HELD, :, 0:INFO]))
    known = jnp.transpose(known, (2, 0, 1, 3)).reshape(TOP, ZL * PEERS, INFO)
    slots = plan(where, known)
    sums = near_part(where, own, rest, near)
    hidden = expert(0, where, own, rest, slots, sums, far[0])
    hidden = expert(1, where, own, rest, slots, sums, far[1], hidden)
    return jnp.transpose(hidden, (0, 2, 1, 3))[None]


def solution(mesh):
    inner = Mesh(mesh.devices.reshape(ZH, X, ZL, Y, C), ("zh", "x", "zl", "y", "c"))
    tokens = P(("zh", "x", "zl", "y", "c"), None)
    in_specs = (tokens, tokens, tokens, P(("zl", "y", "c"), ("zh", "x"), None))
    out_specs = P(("zh", "x"), ("zl", "y", "c"), None, None, None)
    return jax.shard_map(
        shards, mesh=inner, in_specs=in_specs, out_specs=out_specs, check_vma=False
    )
```

```python
import jax
import jax.numpy as jnp
from jax import lax
from jax.experimental import pallas as pl
from jax.experimental.pallas import tpu as pltpu
from jax.sharding import Mesh, PartitionSpec as P

ZH, X, ZL, Y, C = 2, 4, 4, 8, 2
PEERS = Y * C
HELD = 2
CAP = 9
MAIN = CAP - 1
TOP = 8
TOK = 128
D = 2048
FF = 768
KEPT = PEERS * HELD
LEFT = (ZL - 1) * HELD
COLS = HELD * 2 * TOK
SAID = MAIN - HELD
TILE = 256
INFO = 2 * TOK

f32 = jnp.float32
bf16 = jnp.bfloat16


def iota(shape, dim):
    return lax.broadcasted_iota(jnp.int32, shape, dim)


def earlier():
    return (iota((TOK, TOK), 0) < iota((TOK, TOK), 1)).astype(bf16)


def named(ids, experts):
    hit = (ids[0:1, :] == experts).astype(f32)
    for k in range(1, TOP):
        hit = hit + (ids[k : k + 1, :] == experts).astype(f32)
    return hit


def chosen_rows(ids, first):
    kept = (iota((KEPT, TOK), 0) + first).astype(f32)
    hit = named(ids, kept)
    rank = jnp.dot(hit.astype(bf16), earlier(), preferred_element_type=f32)
    place = jnp.where(hit > 0, rank, -1.0)
    slot = iota((KEPT, MAIN, TOK), 1).astype(f32)
    chosen = (place[:, None, :] == slot).astype(f32)
    return chosen.reshape(KEPT * MAIN, TOK).astype(bf16)


def moved_rows(chosen, rows):
    moved = jnp.dot(chosen, rows, preferred_element_type=f32).astype(bf16)
    return moved.reshape(PEERS, HELD, MAIN, rows.shape[1])


def ids_of(block):
    return block[TOK : TOK + TOP, 0:TOK].astype(f32)


def ending_rows(ids, first, b):
    row = iota((PEERS * MAIN, TOK), 0)
    experts = (first + row // MAIN * HELD + row % HELD).astype(f32)
    hit = jnp.where((row % MAIN // HELD + 1) % ZL == b, named(ids, experts), 0.0)
    rank = jnp.dot(hit.astype(bf16), earlier(), preferred_element_type=f32)
    return jnp.where(rank == MAIN, hit, 0.0).astype(bf16)


def own_kernel(zl_ref, block, out_ref, main_ref, tail_ref):
    @pl.when(pl.program_id(0) == 0)
    def _():
        first = zl_ref[0] * KEPT
        main_ref[...] = chosen_rows(ids_of(block), first)
        tail_ref[...] = ending_rows(ids_of(block), first, 0)

    rows = block[0:TOK, :]
    out_ref[:, 0:HELD] = moved_rows(main_ref[...], rows)
    last = jnp.dot(tail_ref[...], rows, preferred_element_type=f32).astype(bf16)
    out_ref[:, HELD] = last.reshape(PEERS, MAIN, rows.shape[1])


def rest_kernel(zl_ref, *refs):
    blocks, (out_ref, main_ref, tail_ref, said_ref) = refs[:ZL], refs[-4:]

    @pl.when(pl.program_id(0) == 0)
    def _():
        first = zl_ref[0] * KEPT
        kept = (iota((KEPT, TOK), 0) + first).astype(f32)
        for b in range(ZL):
            ids = ids_of(blocks[b])
            gates = blocks[b][TOK : TOK + TOP, TOK:INFO].astype(f32)
            gate = jnp.zeros((KEPT, TOK), f32)
            for k in range(TOP):
                gate = gate + jnp.where(ids[k : k + 1, :] == kept, gates[k : k + 1, :], 0.0)
            said_ref[b, :, 0:TOK] = named(ids, kept).astype(bf16)
            said_ref[b, :, TOK:INFO] = gate.astype(bf16)
            if b:
                main_ref[b - 1] = chosen_rows(ids, first)
                tail_ref[b - 1] = ending_rows(ids, first, b)

    width = out_ref.shape[3]
    row, col = iota((PEERS * MAIN, KEPT), 0), iota((PEERS * MAIN, KEPT), 1)
    said = []
    for e in range(HELD):
        pick = (row % MAIN == SAID) & (col == row // MAIN * HELD + e)
        said.append(
            jnp.dot(
                pick.astype(f32).astype(bf16),
                said_ref[pl.program_id(0)],
                preferred_element_type=f32,
            )
        )
    last = jnp.concatenate(said, axis=1)
    for b in range(1, ZL):
        rows = blocks[b][0:TOK, :]
        moved = moved_rows(main_ref[b - 1], rows)
        for e in range(HELD):
            out_ref[:, e * (ZL - 1) + b - 1] = moved[:, e]
        last = last + jnp.dot(tail_ref[b - 1], rows, preferred_element_type=f32)
    out_ref[:, LEFT] = last.astype(bf16).reshape(PEERS, MAIN, width)


def dispatch(zl, blocks, *others):
    whole = len(blocks) == ZL
    tiles = LEFT + 1 if whole else HELD + 1
    scratch = [pltpu.VMEM((KEPT * MAIN, TOK), bf16), pltpu.VMEM((PEERS * MAIN, TOK), bf16)]
    if whole:
        scratch = [
            pltpu.VMEM((ZL - 1, KEPT * MAIN, TOK), bf16),
            pltpu.VMEM((ZL - 1, PEERS * MAIN, TOK), bf16),
            pltpu.VMEM((ZL, KEPT, INFO), bf16),
        ]
    return pl.pallas_call(
        rest_kernel if whole else own_kernel,
        grid_spec=pltpu.PrefetchScalarGridSpec(
            num_scalar_prefetch=1,
            grid=(D // COLS,),
            in_specs=[pl.BlockSpec((TOK + TOP, COLS), lambda n, z: (0, n))] * len(blocks)
            + [pl.BlockSpec(memory_space=pl.ANY)] * len(others),
            out_specs=pl.BlockSpec((PEERS, tiles, MAIN, COLS), lambda n, z: (0, 0, 0, n)),
            scratch_shapes=scratch,
        ),
        out_shape=jax.ShapeDtypeStruct((PEERS, tiles, MAIN, D), bf16),
        compiler_params=pltpu.CompilerParams(vmem_limit_bytes=40 * 1024 * 1024),
        cost_estimate=pl.CostEstimate(
            flops=2 * len(blocks) * 384 * TOK * D,
            bytes_accessed=PEERS * tiles * MAIN * D * 2,
            transcendentals=0,
        ),
    )(zl, *blocks, *others)


def plan_kernel(where_ref, last_ref, gate_ref, sort_ref, sort8_ref):
    blocks = PEERS * ZL
    count = blocks * MAIN
    near_rows = PEERS * MAIN
    rest = (ZL - 1) * MAIN
    zl = where_ref[0]
    out_row, in_row = iota((count, count), 0), iota((count, count), 1)
    late = in_row - near_rows
    peer = jnp.where(late >= 0, late // rest, in_row // MAIN)
    b = jnp.where(late >= 0, late % rest // MAIN + 1, 0)
    source = (zl - b + ZL) % ZL * PEERS + peer
    sort_ref[...] = (out_row == in_row % MAIN * blocks + source).astype(f32).astype(bf16)
    ones = jnp.ones((TOK, TILE), bf16)
    said = last_ref[...].astype(f32).reshape(PEERS, MAIN, D)[:, SAID, :]
    for e in range(HELD):
        starts = [(b * HELD + e) * INFO for b in range(ZL)]
        hit = jnp.concatenate([said[:, at : at + TOK] for at in starts], axis=0)
        gate = jnp.concatenate([said[:, at + TOK : at + INFO] for at in starts], axis=0)
        rank = jnp.dot(hit.astype(bf16), earlier(), preferred_element_type=f32)
        slot = iota((blocks, MAIN, TOK), 1).astype(f32)
        chosen = jnp.where(rank[:, None, :] == slot, gate[:, None, :], 0.0)
        chosen = chosen.reshape(ZL, near_rows, TOK)
        gate_ref[e, 0:near_rows, :] = jnp.dot(
            chosen[0].astype(bf16), ones, preferred_element_type=f32
        )
        others = jnp.concatenate(
            [chosen[b].reshape(PEERS, MAIN, TOK) for b in range(1, ZL)], axis=1
        ).reshape(PEERS * rest, TOK)
        gate_ref[e, near_rows:count, :] = jnp.dot(
            others.astype(bf16), ones, preferred_element_type=f32
        )
        last = jnp.where(rank == MAIN, gate, 0.0).astype(bf16)
        last = jnp.dot(last, ones, preferred_element_type=f32).astype(bf16)
        row, col = iota((blocks * HELD, blocks), 0), iota((blocks * HELD, blocks), 1)
        b = (row // HELD + 1) % ZL
        spread = (col == b * PEERS + row // MAIN).astype(f32).astype(bf16)
        gate_ref[e, count:, :] = jnp.dot(spread, last, preferred_element_type=f32)
        out_row, in_row = iota((blocks, blocks * HELD), 0), iota((blocks, blocks * HELD), 1)
        source = (zl - (in_row // HELD + 1) % ZL + ZL) % ZL * PEERS + in_row // MAIN
        keep = (out_row == source) & (in_row % HELD == e)
        sort8_ref[e] = keep.astype(f32).astype(bf16)


def plan(where, rest):
    blocks = PEERS * ZL
    rows = blocks * (MAIN + HELD)
    shapes = [
        jax.ShapeDtypeStruct((HELD, rows, TILE), f32),
        jax.ShapeDtypeStruct((blocks * MAIN, blocks * MAIN), bf16),
        jax.ShapeDtypeStruct((HELD, blocks, blocks * HELD), bf16),
    ]
    return pl.pallas_call(
        plan_kernel,
        grid_spec=pltpu.PrefetchScalarGridSpec(
            num_scalar_prefetch=1,
            grid=(1,),
            in_specs=[pl.BlockSpec((PEERS, 1, MAIN, D), lambda n, w: (0, LEFT, 0, 0))],
            out_specs=[
                pl.BlockSpec(s.shape, lambda n, w, r=len(s.shape): (0,) * r) for s in shapes
            ],
        ),
        out_shape=shapes,
        compiler_params=pltpu.CompilerParams(vmem_limit_bytes=32 * 1024 * 1024),
        cost_estimate=pl.CostEstimate(flops=10**8, bytes_accessed=10**6, transcendentals=0),
    )(where, rest)


def gather_rows(rows_ref, own_ref, rest_ref, own_last_ref, last_ref):
    at = 0
    half = rows_ref.shape[1]
    for ref in (own_ref, rest_ref):
        count = ref.shape[0] * ref.shape[1] * ref.shape[2]
        rows_ref[at : at + count, :] = ref[...].reshape(count, half)
        at += count
    count = PEERS * MAIN
    mine = iota((count, half), 0) % MAIN >= SAID
    own_last = own_last_ref[...].astype(f32).reshape(count, half)
    last = last_ref[...].astype(f32).reshape(count, half)
    rows_ref[at:, :] = jnp.where(mine, own_last, last).astype(bf16)


def near_kernel(where_ref, own_ref, rest_ref, own_last_ref, last_ref, weights_ref, out_ref, rows_ref):
    @pl.when(pl.program_id(1) == 0)
    def _():
        gather_rows(rows_ref, own_ref, rest_ref, own_last_ref, last_ref)

    weights = weights_ref[...].reshape(D // 2, weights_ref.shape[3])
    out_ref[0] = jnp.dot(rows_ref[...], weights, preferred_element_type=f32)


def near_part(where, own, rest, near):
    rows, half, tile = PEERS * ZL * (MAIN + HELD), D // 2, 2 * TILE
    return pl.pallas_call(
        near_kernel,
        grid_spec=pltpu.PrefetchScalarGridSpec(
            num_scalar_prefetch=1,
            grid=(HELD, 2 * FF // tile),
            in_specs=[
                pl.BlockSpec((PEERS, 1, MAIN, half), lambda e, n, w: (0, e, 0, w[1])),
                pl.BlockSpec((PEERS, ZL - 1, MAIN, half), lambda e, n, w: (0, e, 0, w[1])),
                pl.BlockSpec((PEERS, 1, MAIN, half), lambda e, n, w: (0, HELD, 0, w[1])),
                pl.BlockSpec((PEERS, 1, MAIN, half), lambda e, n, w: (0, LEFT, 0, w[1])),
                pl.BlockSpec((X, 1, D // 8, tile), lambda e, n, w: (0, e, 0, n)),
            ],
            out_specs=pl.BlockSpec((1, rows, tile), lambda e, n, w: (e, 0, n)),
            scratch_shapes=[pltpu.VMEM((rows, half), bf16)],
        ),
        out_shape=jax.ShapeDtypeStruct((HELD, rows, 2 * FF), f32),
        compiler_params=pltpu.CompilerParams(vmem_limit_bytes=60 * 1024 * 1024),
        cost_estimate=pl.CostEstimate(flops=10**11, bytes_accessed=10**7, transcendentals=0),
    )(where, own, rest, own, rest, near)


def expert_kernel(
    where_ref, own_ref, rest_ref, own_last_ref, last_ref, gate_ref, sort_ref, sort8_ref,
    before_ref, up_ref, *refs,
):
    g_refs, u_refs, (out_ref, rows_ref) = refs[:X], refs[X : 2 * X], refs[-2:]
    blocks = PEERS * ZL
    count = blocks * MAIN
    half = D // 2

    @pl.when(pl.program_id(0) == 0)
    def _():
        piece = D // 8
        for d in range(X):
            cols = pl.ds(pl.multiple_of(lax.rem(where_ref[2] - d + X, X) * piece, piece), piece)
            parts = [r.at[:, :, :, cols] for r in (own_ref, rest_ref, own_last_ref, last_ref)]
            gather_rows(rows_ref.at[:, d * piece : (d + 1) * piece], *parts)

    def added(sums_ref, weight_refs):
        weights = jnp.concatenate([ref[...] for ref in weight_refs], axis=0)
        return sums_ref[0] + jnp.dot(rows_ref[...], weights, preferred_element_type=f32)

    before = added(before_ref, g_refs)
    up = added(up_ref, u_refs)
    hidden = (before / (1.0 + jnp.exp(-before)) * up * gate_ref[0]).astype(bf16)
    main = jnp.dot(sort_ref[...], hidden[0:count], preferred_element_type=f32)
    out_ref[0, 0:MAIN] = main.astype(bf16).reshape(MAIN, blocks, TILE)
    last = jnp.dot(sort8_ref[0], hidden[count:], preferred_element_type=f32)
    out_ref[0, MAIN] = last.astype(bf16)


def expert(e, where, own, rest, slots, sums, far, other=None):
    blocks = PEERS * ZL
    tiles = FF // TILE
    rows, half = blocks * (MAIN + HELD), D // 2
    gates, sort, sort8 = slots
    others = [] if other is None else [other]
    return pl.pallas_call(
        expert_kernel,
        grid_spec=pltpu.PrefetchScalarGridSpec(
            num_scalar_prefetch=1,
            grid=(tiles,),
            in_specs=[
                pl.BlockSpec((PEERS, 1, MAIN, half), lambda n, w: (0, e, 0, 1 - w[1])),
                pl.BlockSpec((PEERS, ZL - 1, MAIN, half), lambda n, w: (0, e, 0, 1 - w[1])),
                pl.BlockSpec((PEERS, 1, MAIN, half), lambda n, w: (0, HELD, 0, 1 - w[1])),
                pl.BlockSpec((PEERS, 1, MAIN, half), lambda n, w: (0, LEFT, 0, 1 - w[1])),
                pl.BlockSpec((1, rows, TILE), lambda n, w: (e, 0, 0)),
                pl.BlockSpec(sort.shape, lambda n, w: (0, 0)),
                pl.BlockSpec((1,) + sort8.shape[1:], lambda n, w: (e, 0, 0)),
                pl.BlockSpec((1, rows, TILE), lambda n, w: (e, 0, n)),
                pl.BlockSpec((1, rows, TILE), lambda n, w: (e, 0, n + tiles)),
            ]
            + [pl.BlockSpec((D // 8, TILE), lambda n, w: (0, n))] * X
            + [pl.BlockSpec((D // 8, TILE), lambda n, w: (0, n + tiles))] * X
            + [pl.BlockSpec(memory_space=pl.ANY)] * len(others),
            out_specs=pl.BlockSpec((1, CAP, blocks, TILE), lambda n, w: (e, 0, 0, n)),
            scratch_shapes=[pltpu.VMEM((rows, half), bf16)],
        ),
        out_shape=jax.ShapeDtypeStruct((HELD, CAP, blocks, FF), bf16),
        input_output_aliases={10 + 2 * X: 0} if others else {},
        compiler_params=pltpu.CompilerParams(vmem_limit_bytes=60 * 1024 * 1024),
        cost_estimate=pl.CostEstimate(
            flops=rows * D * 2 * FF, bytes_accessed=10_000_000, transcendentals=10**6
        ),
    )(where, own, rest, own, rest, gates, sort, sort8, sums, sums, *far, *far, *others)


def over(axis, count, block):
    return [block] + [
        lax.ppermute(block, axis, [(i, (i + b) % count) for i in range(count)])
        for b in range(1, count)
    ]


def over_peers(message):
    return lax.all_to_all(message, ("y", "c"), split_axis=0, concat_axis=0, tiled=True)


def take_kernel(*refs):
    refs[-1][...] = refs[0][0]


def marks(*values):
    return [
        lax.slice(v, (0,) * v.ndim, (1,) * (v.ndim - 2) + (8, TOK)).reshape(8, TOK) for v in values
    ]


def take(weights, e, *others):
    shape = weights.shape[1:]
    others = marks(*others)
    return pl.pallas_call(
        take_kernel,
        grid=(1,),
        in_specs=[pl.BlockSpec((1,) + shape, lambda n: (e, 0, 0))]
        + [pl.BlockSpec(memory_space=pl.ANY)] * len(others),
        out_specs=pl.BlockSpec(shape, lambda n: (0, 0)),
        out_shape=jax.ShapeDtypeStruct(shape, weights.dtype),
        cost_estimate=pl.CostEstimate(flops=0, bytes_accessed=1_600_000, transcendentals=0),
    )(weights, *others)


def pass_kernel(*refs):
    pass


def after(value, *others):
    others = marks(*others)
    return pl.pallas_call(
        pass_kernel,
        in_specs=[pl.BlockSpec(memory_space=pl.ANY)] * (1 + len(others)),
        out_specs=pl.BlockSpec(memory_space=pl.ANY),
        out_shape=jax.ShapeDtypeStruct(value.shape, value.dtype),
        input_output_aliases={0: 0},
    )(value, *others)


def shards(moe_rows, expert_ids, expert_gates, expert_weights):
    zh, zl = lax.axis_index("zh"), lax.axis_index("zl")
    where = jnp.stack([zl, zh, lax.axis_index("x")])
    info = jnp.concatenate([expert_ids.T.astype(bf16), expert_gates.T], axis=1)
    packed = jnp.concatenate([moe_rows, jnp.pad(info, ((0, 0), (0, D - INFO)))], axis=0)
    blocks = over("zl", ZL, packed)
    near = lax.all_gather(expert_weights, "x", axis=0)
    own = over_peers(dispatch(zl.reshape(1), [packed]))
    swap = [(0, 1), (1, 0)]
    taken = take(expert_weights, 0, *blocks[1:])
    first = lax.ppermute(taken, "zh", swap)
    rest = over_peers(dispatch(zl.reshape(1), blocks, *marks(own, taken)))
    second = lax.ppermute(take(expert_weights, 1, first), "zh", swap)
    far = [over("x", X, first), over("x", X, second)]
    slots = plan(where, rest)
    sums = near_part(where, own, rest, near)
    hidden = expert(0, where, own, rest, slots, sums, far[0])
    hidden = expert(1, where, own, rest, slots, sums, far[1], hidden)
    return jnp.transpose(hidden, (0, 2, 1, 3))[None]


def solution(mesh):
    inner = Mesh(mesh.devices.reshape(ZH, X, ZL, Y, C), ("zh", "x", "zl", "y", "c"))
    tokens = P(("zh", "x", "zl", "y", "c"), None)
    in_specs = (tokens, tokens, tokens, P(("zl", "y", "c"), ("zh", "x"), None))
    out_specs = P(("zh", "x"), ("zl", "y", "c"), None, None, None)
    return jax.shard_map(
        shards, mesh=inner, in_specs=in_specs, out_specs=out_specs, check_vma=False
    )
```

```python
import functools

import jax
import jax.numpy as jnp
from jax import lax
from jax.experimental import pallas as pl
from jax.experimental.pallas import tpu as pltpu
from jax.sharding import Mesh, PartitionSpec as P

ZH, X, ZL, Y, C = 2, 4, 4, 8, 2
PEERS = Y * C
HELD = 2
CAP = 9
MAIN = CAP - 1
TOP = 8
TOK = 128
D = 2048
FF = 768
KEPT = PEERS * HELD
LEFT = (ZL - 1) * HELD
COLS = HELD * 2 * TOK
SAID = MAIN - HELD
TILE = 256
INFO = 2 * TOK

f32 = jnp.float32
bf16 = jnp.bfloat16


def iota(shape, dim):
    return lax.broadcasted_iota(jnp.int32, shape, dim)


def earlier():
    return (iota((TOK, TOK), 0) < iota((TOK, TOK), 1)).astype(bf16)


def named(ids, experts):
    hit = (ids[0:1, :] == experts).astype(f32)
    for k in range(1, TOP):
        hit = hit + (ids[k : k + 1, :] == experts).astype(f32)
    return hit


def chosen_rows(ids, first):
    kept = (iota((KEPT, TOK), 0) + first).astype(f32)
    hit = named(ids, kept)
    rank = jnp.dot(hit.astype(bf16), earlier(), preferred_element_type=f32)
    place = jnp.where(hit > 0, rank, -1.0)
    slot = iota((KEPT, MAIN, TOK), 1).astype(f32)
    chosen = (place[:, None, :] == slot).astype(f32)
    return chosen.reshape(KEPT * MAIN, TOK).astype(bf16)


def moved_rows(chosen, rows):
    moved = jnp.dot(chosen, rows, preferred_element_type=f32).astype(bf16)
    return moved.reshape(PEERS, HELD, MAIN, rows.shape[1])


def ids_of(block):
    return block[TOK : TOK + TOP, 0:TOK].astype(f32)


def ending_rows(ids, first, b):
    row = iota((PEERS * MAIN, TOK), 0)
    experts = (first + row // MAIN * HELD + row % HELD).astype(f32)
    hit = jnp.where((row % MAIN // HELD + 1) % ZL == b, named(ids, experts), 0.0)
    rank = jnp.dot(hit.astype(bf16), earlier(), preferred_element_type=f32)
    return jnp.where(rank == MAIN, hit, 0.0).astype(bf16)


def own_kernel(zl_ref, block, out_ref, main_ref, tail_ref):
    @pl.when(pl.program_id(0) == 0)
    def _():
        first = zl_ref[0] * KEPT
        main_ref[...] = chosen_rows(ids_of(block), first)
        tail_ref[...] = ending_rows(ids_of(block), first, 0)

    rows = block[0:TOK, :]
    out_ref[:, 0:HELD] = moved_rows(main_ref[...], rows)
    last = jnp.dot(tail_ref[...], rows, preferred_element_type=f32).astype(bf16)
    out_ref[:, HELD] = last.reshape(PEERS, MAIN, rows.shape[1])


def rest_kernel(zl_ref, *refs):
    blocks, (out_ref, main_ref, tail_ref, said_ref) = refs[:ZL], refs[-4:]

    @pl.when(pl.program_id(0) == 0)
    def _():
        first = zl_ref[0] * KEPT
        kept = (iota((KEPT, TOK), 0) + first).astype(f32)
        for b in range(ZL):
            ids = ids_of(blocks[b])
            gates = blocks[b][TOK : TOK + TOP, TOK:INFO].astype(f32)
            gate = jnp.zeros((KEPT, TOK), f32)
            for k in range(TOP):
                gate = gate + jnp.where(ids[k : k + 1, :] == kept, gates[k : k + 1, :], 0.0)
            said_ref[b, :, 0:TOK] = named(ids, kept).astype(bf16)
            said_ref[b, :, TOK:INFO] = gate.astype(bf16)
            if b:
                main_ref[b - 1] = chosen_rows(ids, first)
                tail_ref[b - 1] = ending_rows(ids, first, b)

    width = out_ref.shape[3]
    row, col = iota((PEERS * MAIN, KEPT), 0), iota((PEERS * MAIN, KEPT), 1)
    said = []
    for e in range(HELD):
        pick = (row % MAIN == SAID) & (col == row // MAIN * HELD + e)
        said.append(
            jnp.dot(
                pick.astype(f32).astype(bf16),
                said_ref[pl.program_id(0)],
                preferred_element_type=f32,
            )
        )
    last = jnp.concatenate(said, axis=1)
    for b in range(1, ZL):
        rows = blocks[b][0:TOK, :]
        moved = moved_rows(main_ref[b - 1], rows)
        for e in range(HELD):
            out_ref[:, e * (ZL - 1) + b - 1] = moved[:, e]
        last = last + jnp.dot(tail_ref[b - 1], rows, preferred_element_type=f32)
    out_ref[:, LEFT] = last.astype(bf16).reshape(PEERS, MAIN, width)


def dispatch(zl, blocks, *others):
    whole = len(blocks) == ZL
    tiles = LEFT + 1 if whole else HELD + 1
    scratch = [pltpu.VMEM((KEPT * MAIN, TOK), bf16), pltpu.VMEM((PEERS * MAIN, TOK), bf16)]
    if whole:
        scratch = [
            pltpu.VMEM((ZL - 1, KEPT * MAIN, TOK), bf16),
            pltpu.VMEM((ZL - 1, PEERS * MAIN, TOK), bf16),
            pltpu.VMEM((ZL, KEPT, INFO), bf16),
        ]
    return pl.pallas_call(
        rest_kernel if whole else own_kernel,
        grid_spec=pltpu.PrefetchScalarGridSpec(
            num_scalar_prefetch=1,
            grid=(D // COLS,),
            in_specs=[pl.BlockSpec((TOK + TOP, COLS), lambda n, z: (0, n))] * len(blocks)
            + [pl.BlockSpec(memory_space=pl.ANY)] * len(others),
            out_specs=pl.BlockSpec((PEERS, tiles, MAIN, COLS), lambda n, z: (0, 0, 0, n)),
            scratch_shapes=scratch,
        ),
        out_shape=jax.ShapeDtypeStruct((PEERS, tiles, MAIN, D), bf16),
        compiler_params=pltpu.CompilerParams(vmem_limit_bytes=40 * 1024 * 1024),
        cost_estimate=pl.CostEstimate(
            flops=2 * len(blocks) * 384 * TOK * D,
            bytes_accessed=PEERS * tiles * MAIN * D * 2,
            transcendentals=0,
        ),
    )(zl, *blocks, *others)


def plan_kernel(where_ref, last_ref, gate_ref, sort_ref, sort8_ref):
    blocks = PEERS * ZL
    count = blocks * MAIN
    near_rows = PEERS * MAIN
    rest = (ZL - 1) * MAIN
    zl = where_ref[0]
    out_row, in_row = iota((count, count), 0), iota((count, count), 1)
    late = in_row - near_rows
    peer = jnp.where(late >= 0, late // rest, in_row // MAIN)
    b = jnp.where(late >= 0, late % rest // MAIN + 1, 0)
    source = (zl - b + ZL) % ZL * PEERS + peer
    sort_ref[...] = (out_row == in_row % MAIN * blocks + source).astype(f32).astype(bf16)
    ones = jnp.ones((TOK, TOK), bf16)
    said = last_ref[...].astype(f32).reshape(PEERS, MAIN, D)[:, SAID, :]
    for e in range(HELD):
        starts = [(b * HELD + e) * INFO for b in range(ZL)]
        hit = jnp.concatenate([said[:, at : at + TOK] for at in starts], axis=0)
        gate = jnp.concatenate([said[:, at + TOK : at + INFO] for at in starts], axis=0)
        rank = jnp.dot(hit.astype(bf16), earlier(), preferred_element_type=f32)
        slot = iota((blocks, MAIN, TOK), 1).astype(f32)
        chosen = jnp.where(rank[:, None, :] == slot, gate[:, None, :], 0.0)
        chosen = chosen.reshape(ZL, near_rows, TOK)
        gate_ref[e, 0:near_rows, :] = jnp.dot(
            chosen[0].astype(bf16), ones, preferred_element_type=f32
        ).astype(bf16)
        others = jnp.concatenate(
            [chosen[b].reshape(PEERS, MAIN, TOK) for b in range(1, ZL)], axis=1
        ).reshape(PEERS * rest, TOK)
        gate_ref[e, near_rows:count, :] = jnp.dot(
            others.astype(bf16), ones, preferred_element_type=f32
        ).astype(bf16)
        last = jnp.where(rank == MAIN, gate, 0.0).astype(bf16)
        last = jnp.dot(last, ones, preferred_element_type=f32).astype(bf16)
        row, col = iota((blocks * HELD, blocks), 0), iota((blocks * HELD, blocks), 1)
        b = (row // HELD + 1) % ZL
        spread = (col == b * PEERS + row // MAIN).astype(f32).astype(bf16)
        gate_ref[e, count:, :] = jnp.dot(
            spread, last, preferred_element_type=f32
        ).astype(bf16)
        out_row, in_row = iota((blocks, blocks * HELD), 0), iota((blocks, blocks * HELD), 1)
        source = (zl - (in_row // HELD + 1) % ZL + ZL) % ZL * PEERS + in_row // MAIN
        keep = (out_row == source) & (in_row % HELD == e)
        sort8_ref[e] = keep.astype(f32).astype(bf16)


def plan(where, rest):
    blocks = PEERS * ZL
    rows = blocks * (MAIN + HELD)
    shapes = [
        jax.ShapeDtypeStruct((HELD, rows, TOK), bf16),
        jax.ShapeDtypeStruct((blocks * MAIN, blocks * MAIN), bf16),
        jax.ShapeDtypeStruct((HELD, blocks, blocks * HELD), bf16),
    ]
    return pl.pallas_call(
        plan_kernel,
        grid_spec=pltpu.PrefetchScalarGridSpec(
            num_scalar_prefetch=1,
            grid=(1,),
            in_specs=[pl.BlockSpec((PEERS, 1, MAIN, D), lambda n, w: (0, LEFT, 0, 0))],
            out_specs=[
                pl.BlockSpec(s.shape, lambda n, w, r=len(s.shape): (0,) * r) for s in shapes
            ],
        ),
        out_shape=shapes,
        compiler_params=pltpu.CompilerParams(vmem_limit_bytes=32 * 1024 * 1024),
        cost_estimate=pl.CostEstimate(flops=10**8, bytes_accessed=10**6, transcendentals=0),
    )(where, rest)


def gather_rows(rows_ref, own_ref, rest_ref, own_last_ref, last_ref):
    at = 0
    half = rows_ref.shape[1]
    for ref in (own_ref, rest_ref):
        count = ref.shape[0] * ref.shape[1] * ref.shape[2]
        rows_ref[at : at + count, :] = ref[...].reshape(count, half)
        at += count
    count = PEERS * MAIN
    mine = iota((count, half), 0) % MAIN >= SAID
    own_last = own_last_ref[...].astype(f32).reshape(count, half)
    last = last_ref[...].astype(f32).reshape(count, half)
    rows_ref[at:, :] = jnp.where(mine, own_last, last).astype(bf16)


def expert_kernel(pieces, *refs):
    where_ref, own_ref, rest_ref, own_last_ref, last_ref, gate_ref, sort_ref, sort8_ref = refs[:8]
    near_refs, far_refs, (out_ref, rows_ref) = refs[8:10], refs[10 : 10 + 2 * pieces], refs[-2:]
    blocks = PEERS * ZL
    count = blocks * MAIN
    half, width = D // 2, D // 2 // pieces

    @pl.when(pl.program_id(0) == 0)
    def _():
        zh, x = where_ref[1], where_ref[2]
        moves = [(zh * half, 0, half)]
        for d in range(pieces):
            at = lax.rem(x - d + X, X) if pieces == X else 0
            moves.append(((1 - zh) * half + at * width, half + d * width, width))
        for start, to, wide in moves:
            cols = pl.ds(pl.multiple_of(start, D // 8), wide)
            parts = [r.at[:, :, :, cols] for r in (own_ref, rest_ref, own_last_ref, last_ref)]
            gather_rows(rows_ref.at[:, to : to + wide], *parts)

    near, far = rows_ref[:, 0:half], rows_ref[:, half:]

    def product(near_ref, pieces_refs):
        weights = jnp.concatenate([r[...].reshape(width, TILE) for r in pieces_refs], axis=0)
        return jnp.dot(
            near, near_ref[...].reshape(half, TILE), preferred_element_type=f32
        ) + jnp.dot(far, weights, preferred_element_type=f32)

    before = product(near_refs[0], far_refs[:pieces])
    up = product(near_refs[1], far_refs[pieces:])
    gate = gate_ref[0].astype(f32)
    gate = jnp.concatenate([gate] * (TILE // TOK), axis=1)
    hidden = (before / (1.0 + jnp.exp(-before)) * up * gate).astype(bf16)
    main = jnp.dot(sort_ref[...], hidden[0:count], preferred_element_type=f32)
    out_ref[0, 0:MAIN] = main.astype(bf16).reshape(MAIN, blocks, TILE)
    last = jnp.dot(sort8_ref[0], hidden[count:], preferred_element_type=f32)
    out_ref[0, MAIN] = last.astype(bf16)


def expert(e, where, own, rest, slots, near, far, other=None):
    blocks = PEERS * ZL
    tiles = FF // TILE
    rows = blocks * (MAIN + HELD)
    gates, sort, sort8 = slots
    others = [] if other is None else [other]
    far = [f.reshape(-1, f.shape[-1]) for f in far]
    deep = far[0].shape[0]
    return pl.pallas_call(
        functools.partial(expert_kernel, len(far)),
        grid_spec=pltpu.PrefetchScalarGridSpec(
            num_scalar_prefetch=1,
            grid=(tiles,),
            in_specs=[
                pl.BlockSpec((PEERS, 1, MAIN, D), lambda n, w: (0, e, 0, 0)),
                pl.BlockSpec((PEERS, ZL - 1, MAIN, D), lambda n, w: (0, e, 0, 0)),
                pl.BlockSpec((PEERS, 1, MAIN, D), lambda n, w: (0, HELD, 0, 0)),
                pl.BlockSpec((PEERS, 1, MAIN, D), lambda n, w: (0, LEFT, 0, 0)),
                pl.BlockSpec((1,) + gates.shape[1:], lambda n, w: (e, 0, 0)),
                pl.BlockSpec(sort.shape, lambda n, w: (0, 0)),
                pl.BlockSpec((1,) + sort8.shape[1:], lambda n, w: (e, 0, 0)),
                pl.BlockSpec((X, 1, D // 8, TILE), lambda n, w: (0, e, 0, n)),
                pl.BlockSpec((X, 1, D // 8, TILE), lambda n, w: (0, e, 0, n + tiles)),
            ]
            + [pl.BlockSpec((deep, TILE), lambda n, w: (0, n))] * len(far)
            + [pl.BlockSpec((deep, TILE), lambda n, w: (0, n + tiles))] * len(far)
            + [pl.BlockSpec(memory_space=pl.ANY)] * len(others),
            out_specs=pl.BlockSpec((1, CAP, blocks, TILE), lambda n, w: (e, 0, 0, n)),
            scratch_shapes=[pltpu.VMEM((rows, D), bf16)],
        ),
        out_shape=jax.ShapeDtypeStruct((HELD, CAP, blocks, FF), bf16),
        input_output_aliases={10 + 2 * len(far): 0} if others else {},
        compiler_params=pltpu.CompilerParams(vmem_limit_bytes=60 * 1024 * 1024),
        cost_estimate=pl.CostEstimate(
            flops=3*10**9 if e == 0 else 2 * rows * D * 2 * FF,
            bytes_accessed=10_000_000,
            transcendentals=10**6,
        ),
    )(where, own, rest, own, rest, gates, sort, sort8, near, near, *far, *far, *others)


def over(axis, count, block):
    return [block] + [
        lax.ppermute(block, axis, [(i, (i + b) % count) for i in range(count)])
        for b in range(1, count)
    ]


def over_peers(message):
    return lax.all_to_all(message, ("y", "c"), split_axis=0, concat_axis=0, tiled=True)


def take_kernel(*refs):
    refs[-1][...] = refs[0][0]


def marks(*values):
    return [
        lax.slice(v, (0,) * v.ndim, (1,) * (v.ndim - 2) + (8, TOK)).reshape(8, TOK) for v in values
    ]


def take(weights, e, *others):
    shape = weights.shape[1:]
    others = marks(*others)
    return pl.pallas_call(
        take_kernel,
        grid=(1,),
        in_specs=[pl.BlockSpec((1,) + shape, lambda n: (e, 0, 0))]
        + [pl.BlockSpec(memory_space=pl.ANY)] * len(others),
        out_specs=pl.BlockSpec(shape, lambda n: (0, 0)),
        out_shape=jax.ShapeDtypeStruct(shape, weights.dtype),
        cost_estimate=pl.CostEstimate(flops=0, bytes_accessed=1_600_000, transcendentals=0),
    )(weights, *others)


def pass_kernel(*refs):
    pass


def after(value, *others):
    others = marks(*others)
    return pl.pallas_call(
        pass_kernel,
        in_specs=[pl.BlockSpec(memory_space=pl.ANY)] * (1 + len(others)),
        out_specs=pl.BlockSpec(memory_space=pl.ANY),
        out_shape=jax.ShapeDtypeStruct(value.shape, value.dtype),
        input_output_aliases={0: 0},
    )(value, *others)


def shards(moe_rows, expert_ids, expert_gates, expert_weights):
    zh, zl = lax.axis_index("zh"), lax.axis_index("zl")
    where = jnp.stack([zl, zh, lax.axis_index("x")])
    info = jnp.concatenate([expert_ids.T.astype(bf16), expert_gates.T], axis=1)
    packed = jnp.concatenate([moe_rows, jnp.pad(info, ((0, 0), (0, D - INFO)))], axis=0)
    blocks = over("zl", ZL, packed)
    near = lax.all_gather(expert_weights, "x", axis=0)
    own = over_peers(dispatch(zl.reshape(1), [packed]))
    swap = [(0, 1), (1, 0)]
    taken = take(expert_weights, 0, *blocks[1:])
    first = lax.ppermute(taken, "zh", swap)
    rest = over_peers(dispatch(zl.reshape(1), blocks, *marks(own, taken)))
    second = lax.ppermute(take(expert_weights, 1, first), "zh", swap)
    far = [[lax.all_gather(after(first, near), "x", axis=0)], over("x", X, second)]
    slots = plan(where, rest)
    hidden = expert(0, where, own, rest, slots, near, far[0])
    hidden = expert(1, where, own, rest, slots, near, far[1], hidden)
    return jnp.transpose(hidden, (0, 2, 1, 3))[None]


def solution(mesh):
    inner = Mesh(mesh.devices.reshape(ZH, X, ZL, Y, C), ("zh", "x", "zl", "y", "c"))
    tokens = P(("zh", "x", "zl", "y", "c"), None)
    in_specs = (tokens, tokens, tokens, P(("zl", "y", "c"), ("zh", "x"), None))
    out_specs = P(("zh", "x"), ("zl", "y", "c"), None, None, None)
    return jax.shard_map(
        shards, mesh=inner, in_specs=in_specs, out_specs=out_specs, check_vma=False
    )
```

```python
import functools

import jax
import jax.numpy as jnp
from jax import lax
from jax.experimental import pallas as pl
from jax.experimental.pallas import tpu as pltpu
from jax.sharding import Mesh, PartitionSpec as P

ZH, X, ZL, Y, C = 2, 4, 4, 8, 2
PEERS = Y * C
HELD = 2
CAP = 9
MAIN = CAP - 1
TOP = 8
TOK = 128
D = 2048
FF = 768
KEPT = PEERS * HELD
LEFT = (ZL - 1) * HELD
COLS = HELD * 2 * TOK
SAID = MAIN - HELD
TILE = 256
INFO = 2 * TOK

TAKE_COST = (0, 55 * 10**9)
f32 = jnp.float32
bf16 = jnp.bfloat16


def iota(shape, dim):
    return lax.broadcasted_iota(jnp.int32, shape, dim)


def earlier():
    return (iota((TOK, TOK), 0) < iota((TOK, TOK), 1)).astype(bf16)


def named(ids, experts):
    hit = (ids[0:1, :] == experts).astype(f32)
    for k in range(1, TOP):
        hit = hit + (ids[k : k + 1, :] == experts).astype(f32)
    return hit


def chosen_rows(ids, first):
    kept = (iota((KEPT, TOK), 0) + first).astype(f32)
    hit = named(ids, kept)
    rank = jnp.dot(hit.astype(bf16), earlier(), preferred_element_type=f32)
    place = jnp.where(hit > 0, rank, -1.0)
    slot = iota((KEPT, MAIN, TOK), 1).astype(f32)
    chosen = (place[:, None, :] == slot).astype(f32)
    return chosen.reshape(KEPT * MAIN, TOK).astype(bf16)


def moved_rows(chosen, rows):
    moved = jnp.dot(chosen, rows, preferred_element_type=f32).astype(bf16)
    return moved.reshape(PEERS, HELD, MAIN, rows.shape[1])


def ids_of(block):
    return block[TOK : TOK + TOP, 0:TOK].astype(f32)


def ending_rows(ids, first, b):
    row = iota((PEERS * MAIN, TOK), 0)
    experts = (first + row // MAIN * HELD + row % HELD).astype(f32)
    hit = jnp.where((row % MAIN // HELD + 1) % ZL == b, named(ids, experts), 0.0)
    rank = jnp.dot(hit.astype(bf16), earlier(), preferred_element_type=f32)
    return jnp.where(rank == MAIN, hit, 0.0).astype(bf16)


def own_kernel(zl_ref, block, out_ref, main_ref, tail_ref):
    @pl.when(pl.program_id(0) == 0)
    def _():
        first = zl_ref[0] * KEPT
        main_ref[...] = chosen_rows(ids_of(block), first)
        tail_ref[...] = ending_rows(ids_of(block), first, 0)

    rows = block[0:TOK, :]
    out_ref[:, 0:HELD] = moved_rows(main_ref[...], rows)
    last = jnp.dot(tail_ref[...], rows, preferred_element_type=f32).astype(bf16)
    out_ref[:, HELD] = last.reshape(PEERS, MAIN, rows.shape[1])


def rest_kernel(zl_ref, *refs):
    blocks, (out_ref, main_ref, tail_ref, said_ref) = refs[:ZL], refs[-4:]

    @pl.when(pl.program_id(0) == 0)
    def _():
        first = zl_ref[0] * KEPT
        kept = (iota((KEPT, TOK), 0) + first).astype(f32)
        for b in range(ZL):
            ids = ids_of(blocks[b])
            gates = blocks[b][TOK : TOK + TOP, TOK:INFO].astype(f32)
            gate = jnp.zeros((KEPT, TOK), f32)
            for k in range(TOP):
                gate = gate + jnp.where(ids[k : k + 1, :] == kept, gates[k : k + 1, :], 0.0)
            said_ref[b, :, 0:TOK] = named(ids, kept).astype(bf16)
            said_ref[b, :, TOK:INFO] = gate.astype(bf16)
            if b:
                main_ref[b - 1] = chosen_rows(ids, first)
                tail_ref[b - 1] = ending_rows(ids, first, b)

    width = out_ref.shape[3]
    row, col = iota((PEERS * MAIN, KEPT), 0), iota((PEERS * MAIN, KEPT), 1)
    said = []
    for e in range(HELD):
        pick = (row % MAIN == SAID) & (col == row // MAIN * HELD + e)
        said.append(
            jnp.dot(
                pick.astype(f32).astype(bf16),
                said_ref[pl.program_id(0)],
                preferred_element_type=f32,
            )
        )
    last = jnp.concatenate(said, axis=1)
    for b in range(1, ZL):
        rows = blocks[b][0:TOK, :]
        moved = moved_rows(main_ref[b - 1], rows)
        for e in range(HELD):
            out_ref[:, e * (ZL - 1) + b - 1] = moved[:, e]
        last = last + jnp.dot(tail_ref[b - 1], rows, preferred_element_type=f32)
    out_ref[:, LEFT] = last.astype(bf16).reshape(PEERS, MAIN, width)


def dispatch(zl, blocks, *others):
    whole = len(blocks) == ZL
    tiles = LEFT + 1 if whole else HELD + 1
    scratch = [pltpu.VMEM((KEPT * MAIN, TOK), bf16), pltpu.VMEM((PEERS * MAIN, TOK), bf16)]
    if whole:
        scratch = [
            pltpu.VMEM((ZL - 1, KEPT * MAIN, TOK), bf16),
            pltpu.VMEM((ZL - 1, PEERS * MAIN, TOK), bf16),
            pltpu.VMEM((ZL, KEPT, INFO), bf16),
        ]
    return pl.pallas_call(
        rest_kernel if whole else own_kernel,
        grid_spec=pltpu.PrefetchScalarGridSpec(
            num_scalar_prefetch=1,
            grid=(D // COLS,),
            in_specs=[pl.BlockSpec((TOK + TOP, COLS), lambda n, z: (0, n))] * len(blocks)
            + [pl.BlockSpec(memory_space=pl.ANY)] * len(others),
            out_specs=pl.BlockSpec((PEERS, tiles, MAIN, COLS), lambda n, z: (0, 0, 0, n)),
            scratch_shapes=scratch,
        ),
        out_shape=jax.ShapeDtypeStruct((PEERS, tiles, MAIN, D), bf16),
        compiler_params=pltpu.CompilerParams(vmem_limit_bytes=40 * 1024 * 1024),
        cost_estimate=pl.CostEstimate(
            flops=2 * len(blocks) * 384 * TOK * D,
            bytes_accessed=PEERS * tiles * MAIN * D * 2,
            transcendentals=0,
        ),
    )(zl, *blocks, *others)


def plan_kernel(where_ref, last_ref, gate_ref, sort_ref, sort8_ref):
    blocks = PEERS * ZL
    count = blocks * MAIN
    near_rows = PEERS * MAIN
    rest = (ZL - 1) * MAIN
    zl = where_ref[0]
    out_row, in_row = iota((count, count), 0), iota((count, count), 1)
    late = in_row - near_rows
    peer = jnp.where(late >= 0, late // rest, in_row // MAIN)
    b = jnp.where(late >= 0, late % rest // MAIN + 1, 0)
    source = (zl - b + ZL) % ZL * PEERS + peer
    sort_ref[...] = (out_row == in_row % MAIN * blocks + source).astype(f32).astype(bf16)
    ones = jnp.ones((TOK, TOK), bf16)
    said = last_ref[...].astype(f32).reshape(PEERS, MAIN, D)[:, SAID, :]
    for e in range(HELD):
        starts = [(b * HELD + e) * INFO for b in range(ZL)]
        hit = jnp.concatenate([said[:, at : at + TOK] for at in starts], axis=0)
        gate = jnp.concatenate([said[:, at + TOK : at + INFO] for at in starts], axis=0)
        rank = jnp.dot(hit.astype(bf16), earlier(), preferred_element_type=f32)
        slot = iota((blocks, MAIN, TOK), 1).astype(f32)
        chosen = jnp.where(rank[:, None, :] == slot, gate[:, None, :], 0.0)
        chosen = chosen.reshape(ZL, near_rows, TOK)
        gate_ref[e, 0:near_rows, :] = jnp.dot(
            chosen[0].astype(bf16), ones, preferred_element_type=f32
        ).astype(bf16)
        others = jnp.concatenate(
            [chosen[b].reshape(PEERS, MAIN, TOK) for b in range(1, ZL)], axis=1
        ).reshape(PEERS * rest, TOK)
        gate_ref[e, near_rows:count, :] = jnp.dot(
            others.astype(bf16), ones, preferred_element_type=f32
        ).astype(bf16)
        last = jnp.where(rank == MAIN, gate, 0.0).astype(bf16)
        last = jnp.dot(last, ones, preferred_element_type=f32).astype(bf16)
        row, col = iota((blocks * HELD, blocks), 0), iota((blocks * HELD, blocks), 1)
        b = (row // HELD + 1) % ZL
        spread = (col == b * PEERS + row // MAIN).astype(f32).astype(bf16)
        gate_ref[e, count:, :] = jnp.dot(
            spread, last, preferred_element_type=f32
        ).astype(bf16)
        out_row, in_row = iota((blocks, blocks * HELD), 0), iota((blocks, blocks * HELD), 1)
        source = (zl - (in_row // HELD + 1) % ZL + ZL) % ZL * PEERS + in_row // MAIN
        keep = (out_row == source) & (in_row % HELD == e)
        sort8_ref[e] = keep.astype(f32).astype(bf16)


def plan(where, rest):
    blocks = PEERS * ZL
    rows = blocks * (MAIN + HELD)
    shapes = [
        jax.ShapeDtypeStruct((HELD, rows, TOK), bf16),
        jax.ShapeDtypeStruct((blocks * MAIN, blocks * MAIN), bf16),
        jax.ShapeDtypeStruct((HELD, blocks, blocks * HELD), bf16),
    ]
    return pl.pallas_call(
        plan_kernel,
        grid_spec=pltpu.PrefetchScalarGridSpec(
            num_scalar_prefetch=1,
            grid=(1,),
            in_specs=[pl.BlockSpec((PEERS, 1, MAIN, D), lambda n, w: (0, LEFT, 0, 0))],
            out_specs=[
                pl.BlockSpec(s.shape, lambda n, w, r=len(s.shape): (0,) * r) for s in shapes
            ],
        ),
        out_shape=shapes,
        compiler_params=pltpu.CompilerParams(vmem_limit_bytes=32 * 1024 * 1024),
        cost_estimate=pl.CostEstimate(flops=10**8, bytes_accessed=10**6, transcendentals=0),
    )(where, rest)


def gather_rows(rows_ref, own_ref, rest_ref, own_last_ref, last_ref):
    at = 0
    half = rows_ref.shape[1]
    for ref in (own_ref, rest_ref):
        count = ref.shape[0] * ref.shape[1] * ref.shape[2]
        rows_ref[at : at + count, :] = ref[...].reshape(count, half)
        at += count
    count = PEERS * MAIN
    mine = iota((count, half), 0) % MAIN >= SAID
    own_last = own_last_ref[...].astype(f32).reshape(count, half)
    last = last_ref[...].astype(f32).reshape(count, half)
    rows_ref[at:, :] = jnp.where(mine, own_last, last).astype(bf16)


def expert_kernel(pieces, *refs):
    where_ref, own_ref, rest_ref, own_last_ref, last_ref, gate_ref, sort_ref, sort8_ref = refs[:8]
    near_refs, far_refs, (out_ref, rows_ref) = refs[8:10], refs[10 : 10 + 2 * pieces], refs[-2:]
    blocks = PEERS * ZL
    count = blocks * MAIN
    half, width = D // 2, D // 2 // pieces

    @pl.when(pl.program_id(0) == 0)
    def _():
        zh, x = where_ref[1], where_ref[2]
        moves = [(zh * half, 0, half)]
        for d in range(pieces):
            at = lax.rem(x - d + X, X) if pieces == X else 0
            moves.append(((1 - zh) * half + at * width, half + d * width, width))
        for start, to, wide in moves:
            cols = pl.ds(pl.multiple_of(start, D // 8), wide)
            parts = [r.at[:, :, :, cols] for r in (own_ref, rest_ref, own_last_ref, last_ref)]
            gather_rows(rows_ref.at[:, to : to + wide], *parts)

    near, far = rows_ref[:, 0:half], rows_ref[:, half:]

    def product(near_ref, pieces_refs):
        weights = jnp.concatenate([r[...].reshape(width, TILE) for r in pieces_refs], axis=0)
        return jnp.dot(
            near, near_ref[...].reshape(half, TILE), preferred_element_type=f32
        ) + jnp.dot(far, weights, preferred_element_type=f32)

    before = product(near_refs[0], far_refs[:pieces])
    up = product(near_refs[1], far_refs[pieces:])
    gate = gate_ref[0].astype(f32)
    gate = jnp.concatenate([gate] * (TILE // TOK), axis=1)
    hidden = (before / (1.0 + jnp.exp(-before)) * up * gate).astype(bf16)
    main = jnp.dot(sort_ref[...], hidden[0:count], preferred_element_type=f32)
    out_ref[0, 0:MAIN] = main.astype(bf16).reshape(MAIN, blocks, TILE)
    last = jnp.dot(sort8_ref[0], hidden[count:], preferred_element_type=f32)
    out_ref[0, MAIN] = last.astype(bf16)


def expert(e, where, own, rest, slots, near, far, other=None):
    blocks = PEERS * ZL
    tiles = FF // TILE
    rows = blocks * (MAIN + HELD)
    gates, sort, sort8 = slots
    others = [] if other is None else [other]
    far = [f.reshape(-1, f.shape[-1]) for f in far]
    deep = far[0].shape[0]
    return pl.pallas_call(
        functools.partial(expert_kernel, len(far)),
        grid_spec=pltpu.PrefetchScalarGridSpec(
            num_scalar_prefetch=1,
            grid=(tiles,),
            in_specs=[
                pl.BlockSpec((PEERS, 1, MAIN, D), lambda n, w: (0, e, 0, 0)),
                pl.BlockSpec((PEERS, ZL - 1, MAIN, D), lambda n, w: (0, e, 0, 0)),
                pl.BlockSpec((PEERS, 1, MAIN, D), lambda n, w: (0, HELD, 0, 0)),
                pl.BlockSpec((PEERS, 1, MAIN, D), lambda n, w: (0, LEFT, 0, 0)),
                pl.BlockSpec((1,) + gates.shape[1:], lambda n, w: (e, 0, 0)),
                pl.BlockSpec(sort.shape, lambda n, w: (0, 0)),
                pl.BlockSpec((1,) + sort8.shape[1:], lambda n, w: (e, 0, 0)),
                pl.BlockSpec((X, 1, D // 8, TILE), lambda n, w: (0, e, 0, n)),
                pl.BlockSpec((X, 1, D // 8, TILE), lambda n, w: (0, e, 0, n + tiles)),
            ]
            + [pl.BlockSpec((deep, TILE), lambda n, w: (0, n))] * len(far)
            + [pl.BlockSpec((deep, TILE), lambda n, w: (0, n + tiles))] * len(far)
            + [pl.BlockSpec(memory_space=pl.ANY)] * len(others),
            out_specs=pl.BlockSpec((1, CAP, blocks, TILE), lambda n, w: (e, 0, 0, n)),
            scratch_shapes=[pltpu.VMEM((rows, D), bf16)],
        ),
        out_shape=jax.ShapeDtypeStruct((HELD, CAP, blocks, FF), bf16),
        input_output_aliases={10 + 2 * len(far): 0} if others else {},
        compiler_params=pltpu.CompilerParams(vmem_limit_bytes=60 * 1024 * 1024),
        cost_estimate=pl.CostEstimate(
            flops=3*10**9 if e == 0 else 2 * rows * D * 2 * FF,
            bytes_accessed=10_000_000,
            transcendentals=10**6,
        ),
    )(where, own, rest, own, rest, gates, sort, sort8, near, near, *far, *far, *others)


def over(axis, count, block):
    return [block] + [
        lax.ppermute(block, axis, [(i, (i + b) % count) for i in range(count)])
        for b in range(1, count)
    ]


def over_peers(message):
    return lax.all_to_all(message, ("y", "c"), split_axis=0, concat_axis=0, tiled=True)


def take_kernel(*refs):
    refs[-1][...] = refs[0][0]


def marks(*values):
    return [
        lax.slice(v, (0,) * v.ndim, (1,) * (v.ndim - 2) + (8, TOK)).reshape(8, TOK) for v in values
    ]


def take(weights, e, *others):
    shape = weights.shape[1:]
    others = marks(*others)
    return pl.pallas_call(
        take_kernel,
        grid=(1,),
        in_specs=[pl.BlockSpec((1,) + shape, lambda n: (e, 0, 0))]
        + [pl.BlockSpec(memory_space=pl.ANY)] * len(others),
        out_specs=pl.BlockSpec(shape, lambda n: (0, 0)),
        out_shape=jax.ShapeDtypeStruct(shape, weights.dtype),
        cost_estimate=pl.CostEstimate(flops=TAKE_COST[e], bytes_accessed=1_600_000, transcendentals=0),
    )(weights, *others)


def pass_kernel(*refs):
    pass


def after(value, *others):
    others = marks(*others)
    return pl.pallas_call(
        pass_kernel,
        in_specs=[pl.BlockSpec(memory_space=pl.ANY)] * (1 + len(others)),
        out_specs=pl.BlockSpec(memory_space=pl.ANY),
        out_shape=jax.ShapeDtypeStruct(value.shape, value.dtype),
        input_output_aliases={0: 0},
    )(value, *others)


def shards(moe_rows, expert_ids, expert_gates, expert_weights):
    zh, zl = lax.axis_index("zh"), lax.axis_index("zl")
    where = jnp.stack([zl, zh, lax.axis_index("x")])
    info = jnp.concatenate([expert_ids.T.astype(bf16), expert_gates.T], axis=1)
    packed = jnp.concatenate([moe_rows, jnp.pad(info, ((0, 0), (0, D - INFO)))], axis=0)
    blocks = over("zl", ZL, packed)
    near = lax.all_gather(expert_weights, "x", axis=0)
    own = over_peers(dispatch(zl.reshape(1), [packed]))
    swap = [(0, 1), (1, 0)]
    taken = take(expert_weights, 0, *blocks[1:])
    first = lax.ppermute(taken, "zh", swap)
    rest = over_peers(dispatch(zl.reshape(1), blocks, *marks(own, taken)))
    second = lax.ppermute(take(expert_weights, 1, first), "zh", swap)
    far = [over("x", X, first), over("x", X, second)]
    slots = plan(where, rest)
    hidden = expert(0, where, own, rest, slots, near, far[0])
    hidden = expert(1, where, own, rest, slots, near, far[1], hidden)
    return jnp.transpose(hidden, (0, 2, 1, 3))[None]


def solution(mesh):
    inner = Mesh(mesh.devices.reshape(ZH, X, ZL, Y, C), ("zh", "x", "zl", "y", "c"))
    tokens = P(("zh", "x", "zl", "y", "c"), None)
    in_specs = (tokens, tokens, tokens, P(("zl", "y", "c"), ("zh", "x"), None))
    out_specs = P(("zh", "x"), ("zl", "y", "c"), None, None, None)
    return jax.shard_map(
        shards, mesh=inner, in_specs=in_specs, out_specs=out_specs, check_vma=False
    )
```

```python
import functools

import jax
import jax.numpy as jnp
from jax import lax
from jax.experimental import pallas as pl
from jax.experimental.pallas import tpu as pltpu
from jax.sharding import Mesh, PartitionSpec as P

ZH, X, ZL, Y, C = 2, 4, 4, 8, 2
PEERS = Y * C
HELD = 2
CAP = 9
MAIN = CAP - 1
TOP = 8
TOK = 128
D = 2048
FF = 768
KEPT = PEERS * HELD
LEFT = (ZL - 1) * HELD
COLS = HELD * 2 * TOK
SAID = MAIN - HELD
TILE = 256
INFO = 2 * TOK

TAKE_COST = (40 * 10**9, 0 * 10**9)
f32 = jnp.float32
bf16 = jnp.bfloat16


def iota(shape, dim):
    return lax.broadcasted_iota(jnp.int32, shape, dim)


def earlier():
    return (iota((TOK, TOK), 0) < iota((TOK, TOK), 1)).astype(bf16)


def named(ids, experts):
    hit = (ids[0:1, :] == experts).astype(f32)
    for k in range(1, TOP):
        hit = hit + (ids[k : k + 1, :] == experts).astype(f32)
    return hit


def chosen_rows(ids, first):
    kept = (iota((KEPT, TOK), 0) + first).astype(f32)
    hit = named(ids, kept)
    rank = jnp.dot(hit.astype(bf16), earlier(), preferred_element_type=f32)
    place = jnp.where(hit > 0, rank, -1.0)
    slot = iota((KEPT, MAIN, TOK), 1).astype(f32)
    chosen = (place[:, None, :] == slot).astype(f32)
    return chosen.reshape(KEPT * MAIN, TOK).astype(bf16)


def moved_rows(chosen, rows):
    moved = jnp.dot(chosen, rows, preferred_element_type=f32).astype(bf16)
    return moved.reshape(PEERS, HELD, MAIN, rows.shape[1])


def ids_of(block):
    return block[TOK : TOK + TOP, 0:TOK].astype(f32)


def ending_rows(ids, first, b):
    row = iota((PEERS * MAIN, TOK), 0)
    experts = (first + row // MAIN * HELD + row % HELD).astype(f32)
    hit = jnp.where((row % MAIN // HELD + 1) % ZL == b, named(ids, experts), 0.0)
    rank = jnp.dot(hit.astype(bf16), earlier(), preferred_element_type=f32)
    return jnp.where(rank == MAIN, hit, 0.0).astype(bf16)


def own_kernel(zl_ref, block, out_ref, main_ref, tail_ref):
    @pl.when(pl.program_id(0) == 0)
    def _():
        first = zl_ref[0] * KEPT
        main_ref[...] = chosen_rows(ids_of(block), first)
        tail_ref[...] = ending_rows(ids_of(block), first, 0)

    rows = block[0:TOK, :]
    out_ref[:, 0:HELD] = moved_rows(main_ref[...], rows)
    last = jnp.dot(tail_ref[...], rows, preferred_element_type=f32).astype(bf16)
    out_ref[:, HELD] = last.reshape(PEERS, MAIN, rows.shape[1])


def rest_kernel(zl_ref, *refs):
    blocks, (out_ref, main_ref, tail_ref, said_ref) = refs[:ZL], refs[-4:]

    @pl.when(pl.program_id(0) == 0)
    def _():
        first = zl_ref[0] * KEPT
        kept = (iota((KEPT, TOK), 0) + first).astype(f32)
        for b in range(ZL):
            ids = ids_of(blocks[b])
            gates = blocks[b][TOK : TOK + TOP, TOK:INFO].astype(f32)
            gate = jnp.zeros((KEPT, TOK), f32)
            for k in range(TOP):
                gate = gate + jnp.where(ids[k : k + 1, :] == kept, gates[k : k + 1, :], 0.0)
            said_ref[b, :, 0:TOK] = named(ids, kept).astype(bf16)
            said_ref[b, :, TOK:INFO] = gate.astype(bf16)
            if b:
                main_ref[b - 1] = chosen_rows(ids, first)
                tail_ref[b - 1] = ending_rows(ids, first, b)

    width = out_ref.shape[3]
    row, col = iota((PEERS * MAIN, KEPT), 0), iota((PEERS * MAIN, KEPT), 1)
    said = []
    for e in range(HELD):
        pick = (row % MAIN == SAID) & (col == row // MAIN * HELD + e)
        said.append(
            jnp.dot(
                pick.astype(f32).astype(bf16),
                said_ref[pl.program_id(0)],
                preferred_element_type=f32,
            )
        )
    last = jnp.concatenate(said, axis=1)
    for b in range(1, ZL):
        rows = blocks[b][0:TOK, :]
        moved = moved_rows(main_ref[b - 1], rows)
        for e in range(HELD):
            out_ref[:, e * (ZL - 1) + b - 1] = moved[:, e]
        last = last + jnp.dot(tail_ref[b - 1], rows, preferred_element_type=f32)
    out_ref[:, LEFT] = last.astype(bf16).reshape(PEERS, MAIN, width)


def dispatch(zl, blocks, *others):
    whole = len(blocks) == ZL
    tiles = LEFT + 1 if whole else HELD + 1
    scratch = [pltpu.VMEM((KEPT * MAIN, TOK), bf16), pltpu.VMEM((PEERS * MAIN, TOK), bf16)]
    if whole:
        scratch = [
            pltpu.VMEM((ZL - 1, KEPT * MAIN, TOK), bf16),
            pltpu.VMEM((ZL - 1, PEERS * MAIN, TOK), bf16),
            pltpu.VMEM((ZL, KEPT, INFO), bf16),
        ]
    return pl.pallas_call(
        rest_kernel if whole else own_kernel,
        grid_spec=pltpu.PrefetchScalarGridSpec(
            num_scalar_prefetch=1,
            grid=(D // COLS,),
            in_specs=[pl.BlockSpec((TOK + TOP, COLS), lambda n, z: (0, n))] * len(blocks)
            + [pl.BlockSpec(memory_space=pl.ANY)] * len(others),
            out_specs=pl.BlockSpec((PEERS, tiles, MAIN, COLS), lambda n, z: (0, 0, 0, n)),
            scratch_shapes=scratch,
        ),
        out_shape=jax.ShapeDtypeStruct((PEERS, tiles, MAIN, D), bf16),
        compiler_params=pltpu.CompilerParams(vmem_limit_bytes=40 * 1024 * 1024),
        cost_estimate=pl.CostEstimate(
            flops=2 * len(blocks) * 384 * TOK * D,
            bytes_accessed=PEERS * tiles * MAIN * D * 2,
            transcendentals=0,
        ),
    )(zl, *blocks, *others)


def plan_kernel(where_ref, last_ref, gate_ref, sort_ref, sort8_ref):
    blocks = PEERS * ZL
    count = blocks * MAIN
    near_rows = PEERS * MAIN
    rest = (ZL - 1) * MAIN
    zl = where_ref[0]
    out_row, in_row = iota((count, count), 0), iota((count, count), 1)
    late = in_row - near_rows
    peer = jnp.where(late >= 0, late // rest, in_row // MAIN)
    b = jnp.where(late >= 0, late % rest // MAIN + 1, 0)
    source = (zl - b + ZL) % ZL * PEERS + peer
    sort_ref[...] = (out_row == in_row % MAIN * blocks + source).astype(f32).astype(bf16)
    ones = jnp.ones((TOK, TOK), bf16)
    said = last_ref[...].astype(f32).reshape(PEERS, MAIN, D)[:, SAID, :]
    for e in range(HELD):
        starts = [(b * HELD + e) * INFO for b in range(ZL)]
        hit = jnp.concatenate([said[:, at : at + TOK] for at in starts], axis=0)
        gate = jnp.concatenate([said[:, at + TOK : at + INFO] for at in starts], axis=0)
        rank = jnp.dot(hit.astype(bf16), earlier(), preferred_element_type=f32)
        slot = iota((blocks, MAIN, TOK), 1).astype(f32)
        chosen = jnp.where(rank[:, None, :] == slot, gate[:, None, :], 0.0)
        chosen = chosen.reshape(ZL, near_rows, TOK)
        gate_ref[e, 0:near_rows, :] = jnp.dot(
            chosen[0].astype(bf16), ones, preferred_element_type=f32
        ).astype(bf16)
        others = jnp.concatenate(
            [chosen[b].reshape(PEERS, MAIN, TOK) for b in range(1, ZL)], axis=1
        ).reshape(PEERS * rest, TOK)
        gate_ref[e, near_rows:count, :] = jnp.dot(
            others.astype(bf16), ones, preferred_element_type=f32
        ).astype(bf16)
        last = jnp.where(rank == MAIN, gate, 0.0).astype(bf16)
        last = jnp.dot(last, ones, preferred_element_type=f32).astype(bf16)
        row, col = iota((blocks * HELD, blocks), 0), iota((blocks * HELD, blocks), 1)
        b = (row // HELD + 1) % ZL
        spread = (col == b * PEERS + row // MAIN).astype(f32).astype(bf16)
        gate_ref[e, count:, :] = jnp.dot(
            spread, last, preferred_element_type=f32
        ).astype(bf16)
        out_row, in_row = iota((blocks, blocks * HELD), 0), iota((blocks, blocks * HELD), 1)
        source = (zl - (in_row // HELD + 1) % ZL + ZL) % ZL * PEERS + in_row // MAIN
        keep = (out_row == source) & (in_row % HELD == e)
        sort8_ref[e] = keep.astype(f32).astype(bf16)


def plan(where, rest):
    blocks = PEERS * ZL
    rows = blocks * (MAIN + HELD)
    shapes = [
        jax.ShapeDtypeStruct((HELD, rows, TOK), bf16),
        jax.ShapeDtypeStruct((blocks * MAIN, blocks * MAIN), bf16),
        jax.ShapeDtypeStruct((HELD, blocks, blocks * HELD), bf16),
    ]
    return pl.pallas_call(
        plan_kernel,
        grid_spec=pltpu.PrefetchScalarGridSpec(
            num_scalar_prefetch=1,
            grid=(1,),
            in_specs=[pl.BlockSpec((PEERS, 1, MAIN, D), lambda n, w: (0, LEFT, 0, 0))],
            out_specs=[
                pl.BlockSpec(s.shape, lambda n, w, r=len(s.shape): (0,) * r) for s in shapes
            ],
        ),
        out_shape=shapes,
        compiler_params=pltpu.CompilerParams(vmem_limit_bytes=32 * 1024 * 1024),
        cost_estimate=pl.CostEstimate(flops=10**8, bytes_accessed=10**6, transcendentals=0),
    )(where, rest)


def gather_rows(rows_ref, own_ref, rest_ref, own_last_ref, last_ref):
    at = 0
    half = rows_ref.shape[1]
    for ref in (own_ref, rest_ref):
        count = ref.shape[0] * ref.shape[1] * ref.shape[2]
        rows_ref[at : at + count, :] = ref[...].reshape(count, half)
        at += count
    count = PEERS * MAIN
    mine = iota((count, half), 0) % MAIN >= SAID
    own_last = own_last_ref[...].astype(f32).reshape(count, half)
    last = last_ref[...].astype(f32).reshape(count, half)
    rows_ref[at:, :] = jnp.where(mine, own_last, last).astype(bf16)


def expert_kernel(pieces, *refs):
    where_ref, own_ref, rest_ref, own_last_ref, last_ref, gate_ref, sort_ref, sort8_ref = refs[:8]
    near_refs, far_refs, (out_ref, rows_ref) = refs[8:10], refs[10 : 10 + 2 * pieces], refs[-2:]
    blocks = PEERS * ZL
    count = blocks * MAIN
    half, width = D // 2, D // 2 // pieces

    @pl.when(pl.program_id(0) == 0)
    def _():
        zh, x = where_ref[1], where_ref[2]
        moves = [(zh * half, 0, half)]
        for d in range(pieces):
            at = lax.rem(x - d + X, X) if pieces == X else 0
            moves.append(((1 - zh) * half + at * width, half + d * width, width))
        for start, to, wide in moves:
            cols = pl.ds(pl.multiple_of(start, D // 8), wide)
            parts = [r.at[:, :, :, cols] for r in (own_ref, rest_ref, own_last_ref, last_ref)]
            gather_rows(rows_ref.at[:, to : to + wide], *parts)

    near, far = rows_ref[:, 0:half], rows_ref[:, half:]

    def product(near_ref, pieces_refs):
        weights = jnp.concatenate([r[...].reshape(width, TILE) for r in pieces_refs], axis=0)
        return jnp.dot(
            near, near_ref[...].reshape(half, TILE), preferred_element_type=f32
        ) + jnp.dot(far, weights, preferred_element_type=f32)

    before = product(near_refs[0], far_refs[:pieces])
    up = product(near_refs[1], far_refs[pieces:])
    gate = gate_ref[0].astype(f32)
    gate = jnp.concatenate([gate] * (TILE // TOK), axis=1)
    hidden = (before / (1.0 + jnp.exp(-before)) * up * gate).astype(bf16)
    main = jnp.dot(sort_ref[...], hidden[0:count], preferred_element_type=f32)
    out_ref[0, 0:MAIN] = main.astype(bf16).reshape(MAIN, blocks, TILE)
    last = jnp.dot(sort8_ref[0], hidden[count:], preferred_element_type=f32)
    out_ref[0, MAIN] = last.astype(bf16)


def expert(e, where, own, rest, slots, near, far, other=None):
    blocks = PEERS * ZL
    tiles = FF // TILE
    rows = blocks * (MAIN + HELD)
    gates, sort, sort8 = slots
    others = [] if other is None else [other]
    far = [f.reshape(-1, f.shape[-1]) for f in far]
    deep = far[0].shape[0]
    return pl.pallas_call(
        functools.partial(expert_kernel, len(far)),
        grid_spec=pltpu.PrefetchScalarGridSpec(
            num_scalar_prefetch=1,
            grid=(tiles,),
            in_specs=[
                pl.BlockSpec((PEERS, 1, MAIN, D), lambda n, w: (0, e, 0, 0)),
                pl.BlockSpec((PEERS, ZL - 1, MAIN, D), lambda n, w: (0, e, 0, 0)),
                pl.BlockSpec((PEERS, 1, MAIN, D), lambda n, w: (0, HELD, 0, 0)),
                pl.BlockSpec((PEERS, 1, MAIN, D), lambda n, w: (0, LEFT, 0, 0)),
                pl.BlockSpec((1,) + gates.shape[1:], lambda n, w: (e, 0, 0)),
                pl.BlockSpec(sort.shape, lambda n, w: (0, 0)),
                pl.BlockSpec((1,) + sort8.shape[1:], lambda n, w: (e, 0, 0)),
                pl.BlockSpec((X, 1, D // 8, TILE), lambda n, w: (0, e, 0, n)),
                pl.BlockSpec((X, 1, D // 8, TILE), lambda n, w: (0, e, 0, n + tiles)),
            ]
            + [pl.BlockSpec((deep, TILE), lambda n, w: (0, n))] * len(far)
            + [pl.BlockSpec((deep, TILE), lambda n, w: (0, n + tiles))] * len(far)
            + [pl.BlockSpec(memory_space=pl.ANY)] * len(others),
            out_specs=pl.BlockSpec((1, CAP, blocks, TILE), lambda n, w: (e, 0, 0, n)),
            scratch_shapes=[pltpu.VMEM((rows, D), bf16)],
        ),
        out_shape=jax.ShapeDtypeStruct((HELD, CAP, blocks, FF), bf16),
        input_output_aliases={10 + 2 * len(far): 0} if others else {},
        compiler_params=pltpu.CompilerParams(vmem_limit_bytes=60 * 1024 * 1024),
        cost_estimate=pl.CostEstimate(
            flops=3*10**9 if e == 0 else 2 * rows * D * 2 * FF,
            bytes_accessed=10_000_000,
            transcendentals=10**6,
        ),
    )(where, own, rest, own, rest, gates, sort, sort8, near, near, *far, *far, *others)


def over(axis, count, block):
    return [block] + [
        lax.ppermute(block, axis, [(i, (i + b) % count) for i in range(count)])
        for b in range(1, count)
    ]


def over_peers(message):
    return lax.all_to_all(message, ("y", "c"), split_axis=0, concat_axis=0, tiled=True)


def take_kernel(*refs):
    refs[-1][...] = refs[0][0]


def marks(*values):
    return [
        lax.slice(v, (0,) * v.ndim, (1,) * (v.ndim - 2) + (8, TOK)).reshape(8, TOK) for v in values
    ]


def take(weights, e, *others):
    shape = weights.shape[1:]
    others = marks(*others)
    return pl.pallas_call(
        take_kernel,
        grid=(1,),
        in_specs=[pl.BlockSpec((1,) + shape, lambda n: (e, 0, 0))]
        + [pl.BlockSpec(memory_space=pl.ANY)] * len(others),
        out_specs=pl.BlockSpec(shape, lambda n: (0, 0)),
        out_shape=jax.ShapeDtypeStruct(shape, weights.dtype),
        cost_estimate=pl.CostEstimate(flops=TAKE_COST[e], bytes_accessed=1_600_000, transcendentals=0),
    )(weights, *others)


def pass_kernel(*refs):
    pass


def after(value, *others):
    others = marks(*others)
    return pl.pallas_call(
        pass_kernel,
        in_specs=[pl.BlockSpec(memory_space=pl.ANY)] * (1 + len(others)),
        out_specs=pl.BlockSpec(memory_space=pl.ANY),
        out_shape=jax.ShapeDtypeStruct(value.shape, value.dtype),
        input_output_aliases={0: 0},
    )(value, *others)


def shards(moe_rows, expert_ids, expert_gates, expert_weights):
    zh, zl = lax.axis_index("zh"), lax.axis_index("zl")
    where = jnp.stack([zl, zh, lax.axis_index("x")])
    info = jnp.concatenate([expert_ids.T.astype(bf16), expert_gates.T], axis=1)
    packed = jnp.concatenate([moe_rows, jnp.pad(info, ((0, 0), (0, D - INFO)))], axis=0)
    blocks = over("zl", ZL, packed)
    near = lax.all_gather(expert_weights, "x", axis=0)
    own = over_peers(dispatch(zl.reshape(1), [packed]))
    swap = [(0, 1), (1, 0)]
    taken = take(expert_weights, 0, *blocks[1:])
    first = lax.ppermute(taken, "zh", swap)
    rest = over_peers(dispatch(zl.reshape(1), blocks, *marks(own, taken)))
    second = lax.ppermute(take(expert_weights, 1, first), "zh", swap)
    far = [over("x", X, first), over("x", X, second)]
    slots = plan(where, rest)
    hidden = expert(0, where, own, rest, slots, near, far[0])
    hidden = expert(1, where, own, rest, slots, near, far[1], hidden)
    return jnp.transpose(hidden, (0, 2, 1, 3))[None]


def solution(mesh):
    inner = Mesh(mesh.devices.reshape(ZH, X, ZL, Y, C), ("zh", "x", "zl", "y", "c"))
    tokens = P(("zh", "x", "zl", "y", "c"), None)
    in_specs = (tokens, tokens, tokens, P(("zl", "y", "c"), ("zh", "x"), None))
    out_specs = P(("zh", "x"), ("zl", "y", "c"), None, None, None)
    return jax.shard_map(
        shards, mesh=inner, in_specs=in_specs, out_specs=out_specs, check_vma=False
    )
```

```python
import functools

import jax
import jax.numpy as jnp
from jax import lax
from jax.experimental import pallas as pl
from jax.experimental.pallas import tpu as pltpu
from jax.sharding import Mesh, PartitionSpec as P

ZH, X, ZL, Y, C = 2, 4, 4, 8, 2
PEERS = Y * C
HELD = 2
CAP = 9
MAIN = CAP - 1
TOP = 8
TOK = 128
D = 2048
FF = 768
KEPT = PEERS * HELD
LEFT = (ZL - 1) * HELD
COLS = HELD * 2 * TOK
SAID = MAIN - HELD
TILE = 256
INFO = 2 * TOK

TAKE_COST = (40 * 10**9, 55 * 10**9)
f32 = jnp.float32
bf16 = jnp.bfloat16


def iota(shape, dim):
    return lax.broadcasted_iota(jnp.int32, shape, dim)


def earlier():
    return (iota((TOK, TOK), 0) < iota((TOK, TOK), 1)).astype(bf16)


def named(ids, experts):
    hit = (ids[0:1, :] == experts).astype(f32)
    for k in range(1, TOP):
        hit = hit + (ids[k : k + 1, :] == experts).astype(f32)
    return hit


def chosen_rows(ids, first):
    kept = (iota((KEPT, TOK), 0) + first).astype(f32)
    hit = named(ids, kept)
    rank = jnp.dot(hit.astype(bf16), earlier(), preferred_element_type=f32)
    place = jnp.where(hit > 0, rank, -1.0)
    slot = iota((KEPT, MAIN, TOK), 1).astype(f32)
    chosen = (place[:, None, :] == slot).astype(f32)
    return chosen.reshape(KEPT * MAIN, TOK).astype(bf16)


def moved_rows(chosen, rows):
    moved = jnp.dot(chosen, rows, preferred_element_type=f32).astype(bf16)
    return moved.reshape(PEERS, HELD, MAIN, rows.shape[1])


def ids_of(block):
    return block[TOK : TOK + TOP, 0:TOK].astype(f32)


def ending_rows(ids, first, b):
    row = iota((PEERS * MAIN, TOK), 0)
    experts = (first + row // MAIN * HELD + row % HELD).astype(f32)
    hit = jnp.where((row % MAIN // HELD + 1) % ZL == b, named(ids, experts), 0.0)
    rank = jnp.dot(hit.astype(bf16), earlier(), preferred_element_type=f32)
    return jnp.where(rank == MAIN, hit, 0.0).astype(bf16)


def own_kernel(zl_ref, block, out_ref, main_ref, tail_ref):
    @pl.when(pl.program_id(0) == 0)
    def _():
        first = zl_ref[0] * KEPT
        main_ref[...] = chosen_rows(ids_of(block), first)
        tail_ref[...] = ending_rows(ids_of(block), first, 0)

    rows = block[0:TOK, :]
    out_ref[:, 0:HELD] = moved_rows(main_ref[...], rows)
    last = jnp.dot(tail_ref[...], rows, preferred_element_type=f32).astype(bf16)
    out_ref[:, HELD] = last.reshape(PEERS, MAIN, rows.shape[1])


def rest_kernel(zl_ref, *refs):
    blocks, (out_ref, main_ref, tail_ref, said_ref) = refs[:ZL], refs[-4:]

    @pl.when(pl.program_id(0) == 0)
    def _():
        first = zl_ref[0] * KEPT
        kept = (iota((KEPT, TOK), 0) + first).astype(f32)
        for b in range(ZL):
            ids = ids_of(blocks[b])
            gates = blocks[b][TOK : TOK + TOP, TOK:INFO].astype(f32)
            gate = jnp.zeros((KEPT, TOK), f32)
            for k in range(TOP):
                gate = gate + jnp.where(ids[k : k + 1, :] == kept, gates[k : k + 1, :], 0.0)
            said_ref[b, :, 0:TOK] = named(ids, kept).astype(bf16)
            said_ref[b, :, TOK:INFO] = gate.astype(bf16)
            if b:
                main_ref[b - 1] = chosen_rows(ids, first)
                tail_ref[b - 1] = ending_rows(ids, first, b)

    width = out_ref.shape[3]
    row, col = iota((PEERS * MAIN, KEPT), 0), iota((PEERS * MAIN, KEPT), 1)
    said = []
    for e in range(HELD):
        pick = (row % MAIN == SAID) & (col == row // MAIN * HELD + e)
        said.append(
            jnp.dot(
                pick.astype(f32).astype(bf16),
                said_ref[pl.program_id(0)],
                preferred_element_type=f32,
            )
        )
    last = jnp.concatenate(said, axis=1)
    for b in range(1, ZL):
        rows = blocks[b][0:TOK, :]
        moved = moved_rows(main_ref[b - 1], rows)
        for e in range(HELD):
            out_ref[:, e * (ZL - 1) + b - 1] = moved[:, e]
        last = last + jnp.dot(tail_ref[b - 1], rows, preferred_element_type=f32)
    out_ref[:, LEFT] = last.astype(bf16).reshape(PEERS, MAIN, width)


def dispatch(zl, blocks, *others):
    whole = len(blocks) == ZL
    tiles = LEFT + 1 if whole else HELD + 1
    scratch = [pltpu.VMEM((KEPT * MAIN, TOK), bf16), pltpu.VMEM((PEERS * MAIN, TOK), bf16)]
    if whole:
        scratch = [
            pltpu.VMEM((ZL - 1, KEPT * MAIN, TOK), bf16),
            pltpu.VMEM((ZL - 1, PEERS * MAIN, TOK), bf16),
            pltpu.VMEM((ZL, KEPT, INFO), bf16),
        ]
    return pl.pallas_call(
        rest_kernel if whole else own_kernel,
        grid_spec=pltpu.PrefetchScalarGridSpec(
            num_scalar_prefetch=1,
            grid=(D // COLS,),
            in_specs=[pl.BlockSpec((TOK + TOP, COLS), lambda n, z: (0, n))] * len(blocks)
            + [pl.BlockSpec(memory_space=pl.ANY)] * len(others),
            out_specs=pl.BlockSpec((PEERS, tiles, MAIN, COLS), lambda n, z: (0, 0, 0, n)),
            scratch_shapes=scratch,
        ),
        out_shape=jax.ShapeDtypeStruct((PEERS, tiles, MAIN, D), bf16),
        compiler_params=pltpu.CompilerParams(vmem_limit_bytes=40 * 1024 * 1024),
        cost_estimate=pl.CostEstimate(
            flops=2 * len(blocks) * 384 * TOK * D,
            bytes_accessed=PEERS * tiles * MAIN * D * 2,
            transcendentals=0,
        ),
    )(zl, *blocks, *others)


def plan_kernel(where_ref, last_ref, gate_ref, sort_ref, sort8_ref):
    blocks = PEERS * ZL
    count = blocks * MAIN
    near_rows = PEERS * MAIN
    rest = (ZL - 1) * MAIN
    zl = where_ref[0]
    out_row, in_row = iota((count, count), 0), iota((count, count), 1)
    late = in_row - near_rows
    peer = jnp.where(late >= 0, late // rest, in_row // MAIN)
    b = jnp.where(late >= 0, late % rest // MAIN + 1, 0)
    source = (zl - b + ZL) % ZL * PEERS + peer
    sort_ref[...] = (out_row == in_row % MAIN * blocks + source).astype(f32).astype(bf16)
    ones = jnp.ones((TOK, TOK), bf16)
    said = last_ref[...].astype(f32).reshape(PEERS, MAIN, D)[:, SAID, :]
    for e in range(HELD):
        starts = [(b * HELD + e) * INFO for b in range(ZL)]
        hit = jnp.concatenate([said[:, at : at + TOK] for at in starts], axis=0)
        gate = jnp.concatenate([said[:, at + TOK : at + INFO] for at in starts], axis=0)
        rank = jnp.dot(hit.astype(bf16), earlier(), preferred_element_type=f32)
        slot = iota((blocks, MAIN, TOK), 1).astype(f32)
        chosen = jnp.where(rank[:, None, :] == slot, gate[:, None, :], 0.0)
        chosen = chosen.reshape(ZL, near_rows, TOK)
        gate_ref[e, 0:near_rows, :] = jnp.dot(
            chosen[0].astype(bf16), ones, preferred_element_type=f32
        ).astype(bf16)
        others = jnp.concatenate(
            [chosen[b].reshape(PEERS, MAIN, TOK) for b in range(1, ZL)], axis=1
        ).reshape(PEERS * rest, TOK)
        gate_ref[e, near_rows:count, :] = jnp.dot(
            others.astype(bf16), ones, preferred_element_type=f32
        ).astype(bf16)
        last = jnp.where(rank == MAIN, gate, 0.0).astype(bf16)
        last = jnp.dot(last, ones, preferred_element_type=f32).astype(bf16)
        row, col = iota((blocks * HELD, blocks), 0), iota((blocks * HELD, blocks), 1)
        b = (row // HELD + 1) % ZL
        spread = (col == b * PEERS + row // MAIN).astype(f32).astype(bf16)
        gate_ref[e, count:, :] = jnp.dot(
            spread, last, preferred_element_type=f32
        ).astype(bf16)
        out_row, in_row = iota((blocks, blocks * HELD), 0), iota((blocks, blocks * HELD), 1)
        source = (zl - (in_row // HELD + 1) % ZL + ZL) % ZL * PEERS + in_row // MAIN
        keep = (out_row == source) & (in_row % HELD == e)
        sort8_ref[e] = keep.astype(f32).astype(bf16)


def plan(where, rest):
    blocks = PEERS * ZL
    rows = blocks * (MAIN + HELD)
    shapes = [
        jax.ShapeDtypeStruct((HELD, rows, TOK), bf16),
        jax.ShapeDtypeStruct((blocks * MAIN, blocks * MAIN), bf16),
        jax.ShapeDtypeStruct((HELD, blocks, blocks * HELD), bf16),
    ]
    return pl.pallas_call(
        plan_kernel,
        grid_spec=pltpu.PrefetchScalarGridSpec(
            num_scalar_prefetch=1,
            grid=(1,),
            in_specs=[pl.BlockSpec((PEERS, 1, MAIN, D), lambda n, w: (0, LEFT, 0, 0))],
            out_specs=[
                pl.BlockSpec(s.shape, lambda n, w, r=len(s.shape): (0,) * r) for s in shapes
            ],
        ),
        out_shape=shapes,
        compiler_params=pltpu.CompilerParams(vmem_limit_bytes=32 * 1024 * 1024),
        cost_estimate=pl.CostEstimate(flops=10**8, bytes_accessed=10**6, transcendentals=0),
    )(where, rest)


def gather_rows(rows_ref, own_ref, rest_ref, own_last_ref, last_ref):
    at = 0
    half = rows_ref.shape[1]
    for ref in (own_ref, rest_ref):
        count = ref.shape[0] * ref.shape[1] * ref.shape[2]
        rows_ref[at : at + count, :] = ref[...].reshape(count, half)
        at += count
    count = PEERS * MAIN
    mine = iota((count, half), 0) % MAIN >= SAID
    own_last = own_last_ref[...].astype(f32).reshape(count, half)
    last = last_ref[...].astype(f32).reshape(count, half)
    rows_ref[at:, :] = jnp.where(mine, own_last, last).astype(bf16)


def expert_kernel(pieces, *refs):
    where_ref, own_ref, rest_ref, own_last_ref, last_ref, gate_ref, sort_ref, sort8_ref = refs[:8]
    near_refs, far_refs, (out_ref, rows_ref, sums_ref) = refs[8:10], refs[10:-3], refs[-3:]
    e, n = pl.program_id(0), pl.program_id(1)
    blocks = PEERS * ZL
    count = blocks * MAIN
    half, width = D // 2, D // 2 // pieces

    @pl.when(n == 0)
    def _():
        zh, x = where_ref[1], where_ref[2]
        moves = [(zh * half, 0, half)]
        for d in range(pieces):
            at = lax.rem(x - d + X, X) if pieces == X else 0
            moves.append(((1 - zh) * half + at * width, half + d * width, width))
        for start, to, wide in moves:
            cols = pl.ds(pl.multiple_of(start, D // 8), wide)
            parts = [r.at[:, :, :, cols] for r in (own_ref, rest_ref, own_last_ref, last_ref)]
            gather_rows(rows_ref.at[:, to : to + wide], *parts)

    near, far = rows_ref[:, 0:half], rows_ref[:, half:]

    def product(near_ref, pieces_refs):
        weights = jnp.concatenate([r[...].reshape(width, TILE) for r in pieces_refs], axis=0)
        return jnp.dot(
            near, near_ref[...].reshape(half, TILE), preferred_element_type=f32
        ) + jnp.dot(far, weights, preferred_element_type=f32)

    for mine in range(HELD):

        @pl.when(e == mine)
        def _():
            for part in range(2):
                at = (mine * 2 + part) * pieces
                sums_ref[part] = product(near_refs[part], far_refs[at : at + pieces])

    before, up = sums_ref[0], sums_ref[1]
    gate = gate_ref[0].astype(f32)
    gate = jnp.concatenate([gate] * (TILE // TOK), axis=1)
    hidden = (before / (1.0 + jnp.exp(-before)) * up * gate).astype(bf16)
    main = jnp.dot(sort_ref[...], hidden[0:count], preferred_element_type=f32)
    out_ref[0, 0:MAIN] = main.astype(bf16).reshape(MAIN, blocks, TILE)
    last = jnp.dot(sort8_ref[0], hidden[count:], preferred_element_type=f32)
    out_ref[0, MAIN] = last.astype(bf16)


def experts(where, own, rest, slots, near, far):
    blocks = PEERS * ZL
    tiles = FF // TILE
    rows = blocks * (MAIN + HELD)
    gates, sort, sort8 = slots
    pieces = [p for mine in far for p in mine * 2]
    width = D // 2 // len(far[0])
    steps = [lambda e, n: n * (1 - e) + (tiles - 1) * e, lambda e, n: n * e]
    far_specs = [
        pl.BlockSpec((width, TILE), lambda e, n, w, step=step, at=at: (0, step(e, n) + at))
        for step in steps
        for at in (0, tiles)
        for _ in far[0]
    ]
    return pl.pallas_call(
        functools.partial(expert_kernel, len(far[0])),
        grid_spec=pltpu.PrefetchScalarGridSpec(
            num_scalar_prefetch=1,
            grid=(HELD, tiles),
            in_specs=[
                pl.BlockSpec((PEERS, 1, MAIN, D), lambda e, n, w: (0, e, 0, 0)),
                pl.BlockSpec((PEERS, ZL - 1, MAIN, D), lambda e, n, w: (0, e, 0, 0)),
                pl.BlockSpec((PEERS, 1, MAIN, D), lambda e, n, w: (0, HELD, 0, 0)),
                pl.BlockSpec((PEERS, 1, MAIN, D), lambda e, n, w: (0, LEFT, 0, 0)),
                pl.BlockSpec((1,) + gates.shape[1:], lambda e, n, w: (e, 0, 0)),
                pl.BlockSpec(sort.shape, lambda e, n, w: (0, 0)),
                pl.BlockSpec((1,) + sort8.shape[1:], lambda e, n, w: (e, 0, 0)),
                pl.BlockSpec((X, 1, D // 8, TILE), lambda e, n, w: (0, e, 0, n)),
                pl.BlockSpec((X, 1, D // 8, TILE), lambda e, n, w: (0, e, 0, n + tiles)),
            ]
            + far_specs,
            out_specs=pl.BlockSpec((1, CAP, blocks, TILE), lambda e, n, w: (e, 0, 0, n)),
            scratch_shapes=[pltpu.VMEM((rows, D), bf16), pltpu.VMEM((2, rows, TILE), f32)],
        ),
        out_shape=jax.ShapeDtypeStruct((HELD, CAP, blocks, FF), bf16),
        compiler_params=pltpu.CompilerParams(vmem_limit_bytes=60 * 1024 * 1024),
        cost_estimate=pl.CostEstimate(
            flops=HELD * 2 * rows * D * 2 * FF,
            bytes_accessed=20_000_000,
            transcendentals=10**6,
        ),
    )(where, own, rest, own, rest, gates, sort, sort8, near, near, *pieces)


def over(axis, count, block):
    return [block] + [
        lax.ppermute(block, axis, [(i, (i + b) % count) for i in range(count)])
        for b in range(1, count)
    ]


def over_peers(message):
    return lax.all_to_all(message, ("y", "c"), split_axis=0, concat_axis=0, tiled=True)


def take_kernel(*refs):
    refs[-1][...] = refs[0][0]


def marks(*values):
    return [
        lax.slice(v, (0,) * v.ndim, (1,) * (v.ndim - 2) + (8, TOK)).reshape(8, TOK) for v in values
    ]


def take(weights, e, *others):
    shape = weights.shape[1:]
    others = marks(*others)
    return pl.pallas_call(
        take_kernel,
        grid=(1,),
        in_specs=[pl.BlockSpec((1,) + shape, lambda n: (e, 0, 0))]
        + [pl.BlockSpec(memory_space=pl.ANY)] * len(others),
        out_specs=pl.BlockSpec(shape, lambda n: (0, 0)),
        out_shape=jax.ShapeDtypeStruct(shape, weights.dtype),
        cost_estimate=pl.CostEstimate(flops=TAKE_COST[e], bytes_accessed=1_600_000, transcendentals=0),
    )(weights, *others)


def pass_kernel(*refs):
    pass


def after(value, *others):
    others = marks(*others)
    return pl.pallas_call(
        pass_kernel,
        in_specs=[pl.BlockSpec(memory_space=pl.ANY)] * (1 + len(others)),
        out_specs=pl.BlockSpec(memory_space=pl.ANY),
        out_shape=jax.ShapeDtypeStruct(value.shape, value.dtype),
        input_output_aliases={0: 0},
    )(value, *others)


def shards(moe_rows, expert_ids, expert_gates, expert_weights):
    zh, zl = lax.axis_index("zh"), lax.axis_index("zl")
    where = jnp.stack([zl, zh, lax.axis_index("x")])
    info = jnp.concatenate([expert_ids.T.astype(bf16), expert_gates.T], axis=1)
    packed = jnp.concatenate([moe_rows, jnp.pad(info, ((0, 0), (0, D - INFO)))], axis=0)
    blocks = over("zl", ZL, packed)
    near = lax.all_gather(expert_weights, "x", axis=0)
    own = over_peers(dispatch(zl.reshape(1), [packed]))
    swap = [(0, 1), (1, 0)]
    taken = take(expert_weights, 0, *blocks[1:])
    first = lax.ppermute(taken, "zh", swap)
    rest = over_peers(dispatch(zl.reshape(1), blocks, *marks(own, taken)))
    second = lax.ppermute(take(expert_weights, 1, first), "zh", swap)
    far = [over("x", X, first), over("x", X, second)]
    slots = plan(where, rest)
    hidden = experts(where, own, rest, slots, near, far)
    return jnp.transpose(hidden, (0, 2, 1, 3))[None]


def solution(mesh):
    inner = Mesh(mesh.devices.reshape(ZH, X, ZL, Y, C), ("zh", "x", "zl", "y", "c"))
    tokens = P(("zh", "x", "zl", "y", "c"), None)
    in_specs = (tokens, tokens, tokens, P(("zl", "y", "c"), ("zh", "x"), None))
    out_specs = P(("zh", "x"), ("zl", "y", "c"), None, None, None)
    return jax.shard_map(
        shards, mesh=inner, in_specs=in_specs, out_specs=out_specs, check_vma=False
    )
```

```python
import functools

import jax
import jax.numpy as jnp
from jax import lax
from jax.experimental import pallas as pl
from jax.experimental.pallas import tpu as pltpu
from jax.sharding import Mesh, PartitionSpec as P

ZH, X, ZL, Y, C = 2, 4, 4, 8, 2
PEERS = Y * C
HELD = 2
CAP = 9
MAIN = CAP - 1
TOP = 8
TOK = 128
D = 2048
FF = 768
KEPT = PEERS * HELD
LEFT = (ZL - 1) * HELD
COLS = HELD * 2 * TOK
SAID = MAIN - HELD
TILE = 256
INFO = 2 * TOK

TAKE_COST = (40 * 10**9, 0 * 10**9)
f32 = jnp.float32
bf16 = jnp.bfloat16


def iota(shape, dim):
    return lax.broadcasted_iota(jnp.int32, shape, dim)


def earlier():
    return (iota((TOK, TOK), 0) < iota((TOK, TOK), 1)).astype(bf16)


def named(ids, experts):
    hit = (ids[0:1, :] == experts).astype(f32)
    for k in range(1, TOP):
        hit = hit + (ids[k : k + 1, :] == experts).astype(f32)
    return hit


def chosen_rows(ids, first):
    kept = (iota((KEPT, TOK), 0) + first).astype(f32)
    hit = named(ids, kept)
    rank = jnp.dot(hit.astype(bf16), earlier(), preferred_element_type=f32)
    place = jnp.where(hit > 0, rank, -1.0)
    slot = iota((KEPT, MAIN, TOK), 1).astype(f32)
    chosen = (place[:, None, :] == slot).astype(f32)
    return chosen.reshape(KEPT * MAIN, TOK).astype(bf16)


def moved_rows(chosen, rows):
    moved = jnp.dot(chosen, rows, preferred_element_type=f32).astype(bf16)
    return moved.reshape(PEERS, HELD, MAIN, rows.shape[1])


def ids_of(block):
    return block[TOK : TOK + TOP, 0:TOK].astype(f32)


def ending_rows(ids, first, b):
    row = iota((PEERS * MAIN, TOK), 0)
    experts = (first + row // MAIN * HELD + row % HELD).astype(f32)
    hit = jnp.where((row % MAIN // HELD + 1) % ZL == b, named(ids, experts), 0.0)
    rank = jnp.dot(hit.astype(bf16), earlier(), preferred_element_type=f32)
    return jnp.where(rank == MAIN, hit, 0.0).astype(bf16)


def own_kernel(zl_ref, block, out_ref, main_ref, tail_ref):
    @pl.when(pl.program_id(0) == 0)
    def _():
        first = zl_ref[0] * KEPT
        main_ref[...] = chosen_rows(ids_of(block), first)
        tail_ref[...] = ending_rows(ids_of(block), first, 0)

    rows = block[0:TOK, :]
    out_ref[:, 0:HELD] = moved_rows(main_ref[...], rows)
    last = jnp.dot(tail_ref[...], rows, preferred_element_type=f32).astype(bf16)
    out_ref[:, HELD] = last.reshape(PEERS, MAIN, rows.shape[1])


def rest_kernel(zl_ref, *refs):
    blocks, (out_ref, main_ref, tail_ref, said_ref) = refs[:ZL], refs[-4:]

    @pl.when(pl.program_id(0) == 0)
    def _():
        first = zl_ref[0] * KEPT
        kept = (iota((KEPT, TOK), 0) + first).astype(f32)
        for b in range(ZL):
            ids = ids_of(blocks[b])
            gates = blocks[b][TOK : TOK + TOP, TOK:INFO].astype(f32)
            gate = jnp.zeros((KEPT, TOK), f32)
            for k in range(TOP):
                gate = gate + jnp.where(ids[k : k + 1, :] == kept, gates[k : k + 1, :], 0.0)
            said_ref[b, :, 0:TOK] = named(ids, kept).astype(bf16)
            said_ref[b, :, TOK:INFO] = gate.astype(bf16)
            if b:
                main_ref[b - 1] = chosen_rows(ids, first)
                tail_ref[b - 1] = ending_rows(ids, first, b)

    width = out_ref.shape[3]
    row, col = iota((PEERS * MAIN, KEPT), 0), iota((PEERS * MAIN, KEPT), 1)
    said = []
    for e in range(HELD):
        pick = (row % MAIN == SAID) & (col == row // MAIN * HELD + e)
        said.append(
            jnp.dot(
                pick.astype(f32).astype(bf16),
                said_ref[pl.program_id(0)],
                preferred_element_type=f32,
            )
        )
    last = jnp.concatenate(said, axis=1)
    for b in range(1, ZL):
        rows = blocks[b][0:TOK, :]
        moved = moved_rows(main_ref[b - 1], rows)
        for e in range(HELD):
            out_ref[:, e * (ZL - 1) + b - 1] = moved[:, e]
        last = last + jnp.dot(tail_ref[b - 1], rows, preferred_element_type=f32)
    out_ref[:, LEFT] = last.astype(bf16).reshape(PEERS, MAIN, width)


def dispatch(zl, blocks, *others):
    whole = len(blocks) == ZL
    tiles = LEFT + 1 if whole else HELD + 1
    scratch = [pltpu.VMEM((KEPT * MAIN, TOK), bf16), pltpu.VMEM((PEERS * MAIN, TOK), bf16)]
    if whole:
        scratch = [
            pltpu.VMEM((ZL - 1, KEPT * MAIN, TOK), bf16),
            pltpu.VMEM((ZL - 1, PEERS * MAIN, TOK), bf16),
            pltpu.VMEM((ZL, KEPT, INFO), bf16),
        ]
    return pl.pallas_call(
        rest_kernel if whole else own_kernel,
        grid_spec=pltpu.PrefetchScalarGridSpec(
            num_scalar_prefetch=1,
            grid=(D // COLS,),
            in_specs=[pl.BlockSpec((TOK + TOP, COLS), lambda n, z: (0, n))] * len(blocks)
            + [pl.BlockSpec(memory_space=pl.ANY)] * len(others),
            out_specs=pl.BlockSpec((PEERS, tiles, MAIN, COLS), lambda n, z: (0, 0, 0, n)),
            scratch_shapes=scratch,
        ),
        out_shape=jax.ShapeDtypeStruct((PEERS, tiles, MAIN, D), bf16),
        compiler_params=pltpu.CompilerParams(vmem_limit_bytes=40 * 1024 * 1024),
        cost_estimate=pl.CostEstimate(
            flops=2 * len(blocks) * 384 * TOK * D,
            bytes_accessed=PEERS * tiles * MAIN * D * 2,
            transcendentals=0,
        ),
    )(zl, *blocks, *others)


def plan_kernel(where_ref, last_ref, gate_ref, sort_ref, sort8_ref):
    blocks = PEERS * ZL
    count = blocks * MAIN
    near_rows = PEERS * MAIN
    rest = (ZL - 1) * MAIN
    zl = where_ref[0]
    out_row, in_row = iota((count, count), 0), iota((count, count), 1)
    late = in_row - near_rows
    peer = jnp.where(late >= 0, late // rest, in_row // MAIN)
    b = jnp.where(late >= 0, late % rest // MAIN + 1, 0)
    source = (zl - b + ZL) % ZL * PEERS + peer
    sort_ref[...] = (out_row == in_row % MAIN * blocks + source).astype(f32).astype(bf16)
    ones = jnp.ones((TOK, TOK), bf16)
    said = last_ref[...].astype(f32).reshape(PEERS, MAIN, D)[:, SAID, :]
    for e in range(HELD):
        starts = [(b * HELD + e) * INFO for b in range(ZL)]
        hit = jnp.concatenate([said[:, at : at + TOK] for at in starts], axis=0)
        gate = jnp.concatenate([said[:, at + TOK : at + INFO] for at in starts], axis=0)
        rank = jnp.dot(hit.astype(bf16), earlier(), preferred_element_type=f32)
        slot = iota((blocks, MAIN, TOK), 1).astype(f32)
        chosen = jnp.where(rank[:, None, :] == slot, gate[:, None, :], 0.0)
        chosen = chosen.reshape(ZL, near_rows, TOK)
        gate_ref[e, 0:near_rows, :] = jnp.dot(
            chosen[0].astype(bf16), ones, preferred_element_type=f32
        ).astype(bf16)
        others = jnp.concatenate(
            [chosen[b].reshape(PEERS, MAIN, TOK) for b in range(1, ZL)], axis=1
        ).reshape(PEERS * rest, TOK)
        gate_ref[e, near_rows:count, :] = jnp.dot(
            others.astype(bf16), ones, preferred_element_type=f32
        ).astype(bf16)
        last = jnp.where(rank == MAIN, gate, 0.0).astype(bf16)
        last = jnp.dot(last, ones, preferred_element_type=f32).astype(bf16)
        row, col = iota((blocks * HELD, blocks), 0), iota((blocks * HELD, blocks), 1)
        b = (row // HELD + 1) % ZL
        spread = (col == b * PEERS + row // MAIN).astype(f32).astype(bf16)
        gate_ref[e, count:, :] = jnp.dot(
            spread, last, preferred_element_type=f32
        ).astype(bf16)
        out_row, in_row = iota((blocks, blocks * HELD), 0), iota((blocks, blocks * HELD), 1)
        source = (zl - (in_row // HELD + 1) % ZL + ZL) % ZL * PEERS + in_row // MAIN
        keep = (out_row == source) & (in_row % HELD == e)
        sort8_ref[e] = keep.astype(f32).astype(bf16)


def plan(where, rest):
    blocks = PEERS * ZL
    rows = blocks * (MAIN + HELD)
    shapes = [
        jax.ShapeDtypeStruct((HELD, rows, TOK), bf16),
        jax.ShapeDtypeStruct((blocks * MAIN, blocks * MAIN), bf16),
        jax.ShapeDtypeStruct((HELD, blocks, blocks * HELD), bf16),
    ]
    return pl.pallas_call(
        plan_kernel,
        grid_spec=pltpu.PrefetchScalarGridSpec(
            num_scalar_prefetch=1,
            grid=(1,),
            in_specs=[pl.BlockSpec((PEERS, 1, MAIN, D), lambda n, w: (0, LEFT, 0, 0))],
            out_specs=[
                pl.BlockSpec(s.shape, lambda n, w, r=len(s.shape): (0,) * r) for s in shapes
            ],
        ),
        out_shape=shapes,
        compiler_params=pltpu.CompilerParams(vmem_limit_bytes=32 * 1024 * 1024),
        cost_estimate=pl.CostEstimate(flops=10**8, bytes_accessed=10**6, transcendentals=0),
    )(where, rest)


def gather_rows(rows_ref, own_ref, rest_ref, own_last_ref, last_ref):
    at = 0
    half = rows_ref.shape[1]
    for ref in (own_ref, rest_ref):
        count = ref.shape[0] * ref.shape[1] * ref.shape[2]
        rows_ref[at : at + count, :] = ref[...].reshape(count, half)
        at += count
    count = PEERS * MAIN
    mine = iota((count, half), 0) % MAIN >= SAID
    own_last = own_last_ref[...].astype(f32).reshape(count, half)
    last = last_ref[...].astype(f32).reshape(count, half)
    rows_ref[at:, :] = jnp.where(mine, own_last, last).astype(bf16)


def expert_kernel(pieces, *refs):
    where_ref, own_ref, rest_ref, own_last_ref, last_ref, gate_ref, sort_ref, sort8_ref = refs[:8]
    near_refs, far_refs, (out_ref, rows_ref, sums_ref) = refs[8:10], refs[10:-3], refs[-3:]
    e, n = pl.program_id(0), pl.program_id(1)
    blocks = PEERS * ZL
    count = blocks * MAIN
    half, width = D // 2, D // 2 // pieces

    @pl.when(n == 0)
    def _():
        zh, x = where_ref[1], where_ref[2]
        moves = [(zh * half, 0, half)]
        for d in range(pieces):
            at = lax.rem(x - d + X, X) if pieces == X else 0
            moves.append(((1 - zh) * half + at * width, half + d * width, width))
        for start, to, wide in moves:
            cols = pl.ds(pl.multiple_of(start, D // 8), wide)
            parts = [r.at[:, :, :, cols] for r in (own_ref, rest_ref, own_last_ref, last_ref)]
            gather_rows(rows_ref.at[:, to : to + wide], *parts)

    near, far = rows_ref[:, 0:half], rows_ref[:, half:]

    def product(near_ref, pieces_refs):
        weights = jnp.concatenate([r[...].reshape(width, TILE) for r in pieces_refs], axis=0)
        return jnp.dot(
            near, near_ref[...].reshape(half, TILE), preferred_element_type=f32
        ) + jnp.dot(far, weights, preferred_element_type=f32)

    for mine in range(HELD):

        @pl.when(e == mine)
        def _():
            for part in range(2):
                at = (mine * 2 + part) * pieces
                sums_ref[part] = product(near_refs[part], far_refs[at : at + pieces])

    before, up = sums_ref[0], sums_ref[1]
    gate = gate_ref[0].astype(f32)
    gate = jnp.concatenate([gate] * (TILE // TOK), axis=1)
    hidden = (before / (1.0 + jnp.exp(-before)) * up * gate).astype(bf16)
    main = jnp.dot(sort_ref[...], hidden[0:count], preferred_element_type=f32)
    out_ref[0, 0:MAIN] = main.astype(bf16).reshape(MAIN, blocks, TILE)
    last = jnp.dot(sort8_ref[0], hidden[count:], preferred_element_type=f32)
    out_ref[0, MAIN] = last.astype(bf16)


def experts(where, own, rest, slots, near, far):
    blocks = PEERS * ZL
    tiles = FF // TILE
    rows = blocks * (MAIN + HELD)
    gates, sort, sort8 = slots
    pieces = [p for mine in far for p in mine * 2]
    width = D // 2 // len(far[0])
    steps = [lambda e, n: n * (1 - e) + (tiles - 1) * e, lambda e, n: n * e]
    far_specs = [
        pl.BlockSpec((width, TILE), lambda e, n, w, step=step, at=at: (0, step(e, n) + at))
        for step in steps
        for at in (0, tiles)
        for _ in far[0]
    ]
    return pl.pallas_call(
        functools.partial(expert_kernel, len(far[0])),
        grid_spec=pltpu.PrefetchScalarGridSpec(
            num_scalar_prefetch=1,
            grid=(HELD, tiles),
            in_specs=[
                pl.BlockSpec((PEERS, 1, MAIN, D), lambda e, n, w: (0, e, 0, 0)),
                pl.BlockSpec((PEERS, ZL - 1, MAIN, D), lambda e, n, w: (0, e, 0, 0)),
                pl.BlockSpec((PEERS, 1, MAIN, D), lambda e, n, w: (0, HELD, 0, 0)),
                pl.BlockSpec((PEERS, 1, MAIN, D), lambda e, n, w: (0, LEFT, 0, 0)),
                pl.BlockSpec((1,) + gates.shape[1:], lambda e, n, w: (e, 0, 0)),
                pl.BlockSpec(sort.shape, lambda e, n, w: (0, 0)),
                pl.BlockSpec((1,) + sort8.shape[1:], lambda e, n, w: (e, 0, 0)),
                pl.BlockSpec((X, 1, D // 8, TILE), lambda e, n, w: (0, e, 0, n)),
                pl.BlockSpec((X, 1, D // 8, TILE), lambda e, n, w: (0, e, 0, n + tiles)),
            ]
            + far_specs,
            out_specs=pl.BlockSpec((1, CAP, blocks, TILE), lambda e, n, w: (e, 0, 0, n)),
            scratch_shapes=[pltpu.VMEM((rows, D), bf16), pltpu.VMEM((2, rows, TILE), f32)],
        ),
        out_shape=jax.ShapeDtypeStruct((HELD, CAP, blocks, FF), bf16),
        compiler_params=pltpu.CompilerParams(vmem_limit_bytes=60 * 1024 * 1024),
        cost_estimate=pl.CostEstimate(
            flops=HELD * 2 * rows * D * 2 * FF,
            bytes_accessed=20_000_000,
            transcendentals=10**6,
        ),
    )(where, own, rest, own, rest, gates, sort, sort8, near, near, *pieces)


def over(axis, count, block):
    return [block] + [
        lax.ppermute(block, axis, [(i, (i + b) % count) for i in range(count)])
        for b in range(1, count)
    ]


def over_peers(message):
    return lax.all_to_all(message, ("y", "c"), split_axis=0, concat_axis=0, tiled=True)


def take_kernel(*refs):
    refs[-1][...] = refs[0][0]


def marks(*values):
    return [
        lax.slice(v, (0,) * v.ndim, (1,) * (v.ndim - 2) + (8, TOK)).reshape(8, TOK) for v in values
    ]


def take(weights, e, *others):
    shape = weights.shape[1:]
    others = marks(*others)
    return pl.pallas_call(
        take_kernel,
        grid=(1,),
        in_specs=[pl.BlockSpec((1,) + shape, lambda n: (e, 0, 0))]
        + [pl.BlockSpec(memory_space=pl.ANY)] * len(others),
        out_specs=pl.BlockSpec(shape, lambda n: (0, 0)),
        out_shape=jax.ShapeDtypeStruct(shape, weights.dtype),
        cost_estimate=pl.CostEstimate(flops=TAKE_COST[e], bytes_accessed=1_600_000, transcendentals=0),
    )(weights, *others)


def pass_kernel(*refs):
    pass


def after(value, *others):
    others = marks(*others)
    return pl.pallas_call(
        pass_kernel,
        in_specs=[pl.BlockSpec(memory_space=pl.ANY)] * (1 + len(others)),
        out_specs=pl.BlockSpec(memory_space=pl.ANY),
        out_shape=jax.ShapeDtypeStruct(value.shape, value.dtype),
        input_output_aliases={0: 0},
    )(value, *others)


def shards(moe_rows, expert_ids, expert_gates, expert_weights):
    zh, zl = lax.axis_index("zh"), lax.axis_index("zl")
    where = jnp.stack([zl, zh, lax.axis_index("x")])
    info = jnp.concatenate([expert_ids.T.astype(bf16), expert_gates.T], axis=1)
    packed = jnp.concatenate([moe_rows, jnp.pad(info, ((0, 0), (0, D - INFO)))], axis=0)
    blocks = over("zl", ZL, packed)
    near = lax.all_gather(expert_weights, "x", axis=0)
    own = over_peers(dispatch(zl.reshape(1), [packed]))
    swap = [(0, 1), (1, 0)]
    taken = take(expert_weights, 0, *blocks[1:])
    first = lax.ppermute(taken, "zh", swap)
    rest = over_peers(dispatch(zl.reshape(1), blocks, *marks(own, taken)))
    second = lax.ppermute(take(expert_weights, 1, first), "zh", swap)
    far = [over("x", X, first), over("x", X, second)]
    slots = plan(where, rest)
    hidden = experts(where, own, rest, slots, near, far)
    return jnp.transpose(hidden, (0, 2, 1, 3))[None]


def solution(mesh):
    inner = Mesh(mesh.devices.reshape(ZH, X, ZL, Y, C), ("zh", "x", "zl", "y", "c"))
    tokens = P(("zh", "x", "zl", "y", "c"), None)
    in_specs = (tokens, tokens, tokens, P(("zl", "y", "c"), ("zh", "x"), None))
    out_specs = P(("zh", "x"), ("zl", "y", "c"), None, None, None)
    return jax.shard_map(
        shards, mesh=inner, in_specs=in_specs, out_specs=out_specs, check_vma=False
    )
```

```python
import functools

import jax
import jax.numpy as jnp
from jax import lax
from jax.experimental import pallas as pl
from jax.experimental.pallas import tpu as pltpu
from jax.sharding import Mesh, PartitionSpec as P

ZH, X, ZL, Y, C = 2, 4, 4, 8, 2
PEERS = Y * C
HELD = 2
CAP = 9
MAIN = CAP - 1
TOP = 8
TOK = 128
D = 2048
FF = 768
KEPT = PEERS * HELD
LEFT = (ZL - 1) * HELD
COLS = HELD * 2 * TOK
SAID = MAIN - HELD
TILE = 256
INFO = 2 * TOK

TAKE_COST = (40 * 10**9, 55 * 10**9)
f32 = jnp.float32
bf16 = jnp.bfloat16


def iota(shape, dim):
    return lax.broadcasted_iota(jnp.int32, shape, dim)


def earlier():
    return (iota((TOK, TOK), 0) < iota((TOK, TOK), 1)).astype(bf16)


def named(ids, experts):
    hit = (ids[0:1, :] == experts).astype(f32)
    for k in range(1, TOP):
        hit = hit + (ids[k : k + 1, :] == experts).astype(f32)
    return hit


def chosen_rows(ids, first):
    kept = (iota((KEPT, TOK), 0) + first).astype(f32)
    hit = named(ids, kept)
    rank = jnp.dot(hit.astype(bf16), earlier(), preferred_element_type=f32)
    place = jnp.where(hit > 0, rank, -1.0)
    slot = iota((KEPT, MAIN, TOK), 1).astype(f32)
    chosen = (place[:, None, :] == slot).astype(f32)
    return chosen.reshape(KEPT * MAIN, TOK).astype(bf16)


def moved_rows(chosen, rows):
    moved = jnp.dot(chosen, rows, preferred_element_type=f32).astype(bf16)
    return moved.reshape(PEERS, HELD, MAIN, rows.shape[1])


def ids_of(block):
    return block[TOK : TOK + TOP, 0:TOK].astype(f32)


def ending_rows(ids, first, b):
    row = iota((PEERS * MAIN, TOK), 0)
    experts = (first + row // MAIN * HELD + row % HELD).astype(f32)
    hit = jnp.where((row % MAIN // HELD + 1) % ZL == b, named(ids, experts), 0.0)
    rank = jnp.dot(hit.astype(bf16), earlier(), preferred_element_type=f32)
    return jnp.where(rank == MAIN, hit, 0.0).astype(bf16)


def own_kernel(zl_ref, block, out_ref, main_ref, tail_ref):
    @pl.when(pl.program_id(0) == 0)
    def _():
        first = zl_ref[0] * KEPT
        main_ref[...] = chosen_rows(ids_of(block), first)
        tail_ref[...] = ending_rows(ids_of(block), first, 0)

    rows = block[0:TOK, :]
    out_ref[:, 0:HELD] = moved_rows(main_ref[...], rows)
    last = jnp.dot(tail_ref[...], rows, preferred_element_type=f32).astype(bf16)
    out_ref[:, HELD] = last.reshape(PEERS, MAIN, rows.shape[1])


def rest_kernel(zl_ref, *refs):
    blocks, (out_ref, main_ref, tail_ref, said_ref) = refs[:ZL], refs[-4:]

    @pl.when(pl.program_id(0) == 0)
    def _():
        first = zl_ref[0] * KEPT
        kept = (iota((KEPT, TOK), 0) + first).astype(f32)
        for b in range(ZL):
            ids = ids_of(blocks[b])
            gates = blocks[b][TOK : TOK + TOP, TOK:INFO].astype(f32)
            gate = jnp.zeros((KEPT, TOK), f32)
            for k in range(TOP):
                gate = gate + jnp.where(ids[k : k + 1, :] == kept, gates[k : k + 1, :], 0.0)
            said_ref[b, :, 0:TOK] = named(ids, kept).astype(bf16)
            said_ref[b, :, TOK:INFO] = gate.astype(bf16)
            if b:
                main_ref[b - 1] = chosen_rows(ids, first)
                tail_ref[b - 1] = ending_rows(ids, first, b)

    width = out_ref.shape[3]
    row, col = iota((PEERS * MAIN, KEPT), 0), iota((PEERS * MAIN, KEPT), 1)
    said = []
    for e in range(HELD):
        pick = (row % MAIN == SAID) & (col == row // MAIN * HELD + e)
        said.append(
            jnp.dot(
                pick.astype(f32).astype(bf16),
                said_ref[pl.program_id(0)],
                preferred_element_type=f32,
            )
        )
    last = jnp.concatenate(said, axis=1)
    for b in range(1, ZL):
        rows = blocks[b][0:TOK, :]
        moved = moved_rows(main_ref[b - 1], rows)
        for e in range(HELD):
            out_ref[:, e * (ZL - 1) + b - 1] = moved[:, e]
        last = last + jnp.dot(tail_ref[b - 1], rows, preferred_element_type=f32)
    out_ref[:, LEFT] = last.astype(bf16).reshape(PEERS, MAIN, width)


def dispatch(zl, blocks, *others):
    whole = len(blocks) == ZL
    tiles = LEFT + 1 if whole else HELD + 1
    scratch = [pltpu.VMEM((KEPT * MAIN, TOK), bf16), pltpu.VMEM((PEERS * MAIN, TOK), bf16)]
    if whole:
        scratch = [
            pltpu.VMEM((ZL - 1, KEPT * MAIN, TOK), bf16),
            pltpu.VMEM((ZL - 1, PEERS * MAIN, TOK), bf16),
            pltpu.VMEM((ZL, KEPT, INFO), bf16),
        ]
    return pl.pallas_call(
        rest_kernel if whole else own_kernel,
        grid_spec=pltpu.PrefetchScalarGridSpec(
            num_scalar_prefetch=1,
            grid=(D // COLS,),
            in_specs=[pl.BlockSpec((TOK + TOP, COLS), lambda n, z: (0, n))] * len(blocks)
            + [pl.BlockSpec(memory_space=pl.ANY)] * len(others),
            out_specs=pl.BlockSpec((PEERS, tiles, MAIN, COLS), lambda n, z: (0, 0, 0, n)),
            scratch_shapes=scratch,
        ),
        out_shape=jax.ShapeDtypeStruct((PEERS, tiles, MAIN, D), bf16),
        compiler_params=pltpu.CompilerParams(vmem_limit_bytes=40 * 1024 * 1024),
        cost_estimate=pl.CostEstimate(
            flops=2 * len(blocks) * 384 * TOK * D,
            bytes_accessed=PEERS * tiles * MAIN * D * 2,
            transcendentals=0,
        ),
    )(zl, *blocks, *others)


def plan_kernel(where_ref, last_ref, gate_ref, sort_ref, sort8_ref):
    blocks = PEERS * ZL
    count = blocks * MAIN
    near_rows = PEERS * MAIN
    rest = (ZL - 1) * MAIN
    zl = where_ref[0]
    out_row, in_row = iota((count, count), 0), iota((count, count), 1)
    late = in_row - near_rows
    peer = jnp.where(late >= 0, late // rest, in_row // MAIN)
    b = jnp.where(late >= 0, late % rest // MAIN + 1, 0)
    source = (zl - b + ZL) % ZL * PEERS + peer
    sort_ref[...] = (out_row == in_row % MAIN * blocks + source).astype(f32).astype(bf16)
    ones = jnp.ones((TOK, TOK), bf16)
    said = last_ref[...].astype(f32).reshape(PEERS, MAIN, D)[:, SAID, :]
    for e in range(HELD):
        starts = [(b * HELD + e) * INFO for b in range(ZL)]
        hit = jnp.concatenate([said[:, at : at + TOK] for at in starts], axis=0)
        gate = jnp.concatenate([said[:, at + TOK : at + INFO] for at in starts], axis=0)
        rank = jnp.dot(hit.astype(bf16), earlier(), preferred_element_type=f32)
        slot = iota((blocks, MAIN, TOK), 1).astype(f32)
        chosen = jnp.where(rank[:, None, :] == slot, gate[:, None, :], 0.0)
        chosen = chosen.reshape(ZL, near_rows, TOK)
        gate_ref[e, 0:near_rows, :] = jnp.dot(
            chosen[0].astype(bf16), ones, preferred_element_type=f32
        ).astype(bf16)
        others = jnp.concatenate(
            [chosen[b].reshape(PEERS, MAIN, TOK) for b in range(1, ZL)], axis=1
        ).reshape(PEERS * rest, TOK)
        gate_ref[e, near_rows:count, :] = jnp.dot(
            others.astype(bf16), ones, preferred_element_type=f32
        ).astype(bf16)
        last = jnp.where(rank == MAIN, gate, 0.0).astype(bf16)
        last = jnp.dot(last, ones, preferred_element_type=f32).astype(bf16)
        row, col = iota((blocks * HELD, blocks), 0), iota((blocks * HELD, blocks), 1)
        b = (row // HELD + 1) % ZL
        spread = (col == b * PEERS + row // MAIN).astype(f32).astype(bf16)
        gate_ref[e, count:, :] = jnp.dot(
            spread, last, preferred_element_type=f32
        ).astype(bf16)
        out_row, in_row = iota((blocks, blocks * HELD), 0), iota((blocks, blocks * HELD), 1)
        source = (zl - (in_row // HELD + 1) % ZL + ZL) % ZL * PEERS + in_row // MAIN
        keep = (out_row == source) & (in_row % HELD == e)
        sort8_ref[e] = keep.astype(f32).astype(bf16)


def plan(where, rest):
    blocks = PEERS * ZL
    rows = blocks * (MAIN + HELD)
    shapes = [
        jax.ShapeDtypeStruct((HELD, rows, TOK), bf16),
        jax.ShapeDtypeStruct((blocks * MAIN, blocks * MAIN), bf16),
        jax.ShapeDtypeStruct((HELD, blocks, blocks * HELD), bf16),
    ]
    return pl.pallas_call(
        plan_kernel,
        grid_spec=pltpu.PrefetchScalarGridSpec(
            num_scalar_prefetch=1,
            grid=(1,),
            in_specs=[pl.BlockSpec((PEERS, 1, MAIN, D), lambda n, w: (0, LEFT, 0, 0))],
            out_specs=[
                pl.BlockSpec(s.shape, lambda n, w, r=len(s.shape): (0,) * r) for s in shapes
            ],
        ),
        out_shape=shapes,
        compiler_params=pltpu.CompilerParams(vmem_limit_bytes=32 * 1024 * 1024),
        cost_estimate=pl.CostEstimate(flops=10**8, bytes_accessed=10**6, transcendentals=0),
    )(where, rest)


def gather_rows(rows_ref, own_ref, rest_ref, own_last_ref, last_ref):
    at = 0
    half = rows_ref.shape[1]
    for ref in (own_ref, rest_ref):
        count = ref.shape[0] * ref.shape[1] * ref.shape[2]
        rows_ref[at : at + count, :] = ref[...].reshape(count, half)
        at += count
    count = PEERS * MAIN
    mine = iota((count, half), 0) % MAIN >= SAID
    own_last = own_last_ref[...].astype(f32).reshape(count, half)
    last = last_ref[...].astype(f32).reshape(count, half)
    rows_ref[at:, :] = jnp.where(mine, own_last, last).astype(bf16)


def expert_kernel(pieces, *refs):
    where_ref, own_ref, rest_ref, own_last_ref, last_ref, gate_ref, sort_ref, sort8_ref = refs[:8]
    near_refs, far_refs, (out_ref, rows_ref) = refs[8:10], refs[10 : 10 + 2 * pieces], refs[-2:]
    blocks = PEERS * ZL
    count = blocks * MAIN
    half, width = D // 2, D // 2 // pieces

    @pl.when(pl.program_id(0) == 0)
    def _():
        zh, x = where_ref[1], where_ref[2]
        moves = [(zh * half, 0, half)]
        for d in range(pieces):
            at = lax.rem(x - d + X, X) if pieces == X else 0
            moves.append(((1 - zh) * half + at * width, half + d * width, width))
        for start, to, wide in moves:
            cols = pl.ds(pl.multiple_of(start, D // 8), wide)
            parts = [r.at[:, :, :, cols] for r in (own_ref, rest_ref, own_last_ref, last_ref)]
            gather_rows(rows_ref.at[:, to : to + wide], *parts)

    near, far = rows_ref[:, 0:half], rows_ref[:, half:]

    def product(near_ref, pieces_refs):
        weights = jnp.concatenate([r[...].reshape(width, TILE) for r in pieces_refs], axis=0)
        return jnp.dot(
            near, near_ref[...].reshape(half, TILE), preferred_element_type=f32
        ) + jnp.dot(far, weights, preferred_element_type=f32)

    before = product(near_refs[0], far_refs[:pieces])
    up = product(near_refs[1], far_refs[pieces:])
    gate = gate_ref[0].astype(f32)
    gate = jnp.concatenate([gate] * (TILE // TOK), axis=1)
    hidden = (before / (1.0 + jnp.exp(-before)) * up * gate).astype(bf16)
    main = jnp.dot(sort_ref[...], hidden[0:count], preferred_element_type=f32)
    out_ref[0, 0:MAIN] = main.astype(bf16).reshape(MAIN, blocks, TILE)
    last = jnp.dot(sort8_ref[0], hidden[count:], preferred_element_type=f32)
    out_ref[0, MAIN] = last.astype(bf16)


def expert(e, where, own, rest, slots, near, far, other=None):
    blocks = PEERS * ZL
    tiles = FF // TILE
    rows = blocks * (MAIN + HELD)
    gates, sort, sort8 = slots
    others = [] if other is None else [other]
    far = [f.reshape(-1, f.shape[-1]) for f in far]
    deep = far[0].shape[0]
    return pl.pallas_call(
        functools.partial(expert_kernel, len(far)),
        grid_spec=pltpu.PrefetchScalarGridSpec(
            num_scalar_prefetch=1,
            grid=(tiles,),
            in_specs=[
                pl.BlockSpec((PEERS, 1, MAIN, D), lambda n, w: (0, e, 0, 0)),
                pl.BlockSpec((PEERS, ZL - 1, MAIN, D), lambda n, w: (0, e, 0, 0)),
                pl.BlockSpec((PEERS, 1, MAIN, D), lambda n, w: (0, HELD, 0, 0)),
                pl.BlockSpec((PEERS, 1, MAIN, D), lambda n, w: (0, LEFT, 0, 0)),
                pl.BlockSpec((1,) + gates.shape[1:], lambda n, w: (e, 0, 0)),
                pl.BlockSpec(sort.shape, lambda n, w: (0, 0)),
                pl.BlockSpec((1,) + sort8.shape[1:], lambda n, w: (e, 0, 0)),
                pl.BlockSpec((X, 1, D // 8, TILE), lambda n, w: (0, e, 0, n)),
                pl.BlockSpec((X, 1, D // 8, TILE), lambda n, w: (0, e, 0, n + tiles)),
            ]
            + [pl.BlockSpec((deep, TILE), lambda n, w: (0, n))] * len(far)
            + [pl.BlockSpec((deep, TILE), lambda n, w: (0, n + tiles))] * len(far)
            + [pl.BlockSpec(memory_space=pl.ANY)] * len(others),
            out_specs=pl.BlockSpec((1, CAP, blocks, TILE), lambda n, w: (e, 0, 0, n)),
            scratch_shapes=[pltpu.VMEM((rows, D), bf16)],
        ),
        out_shape=jax.ShapeDtypeStruct((HELD, CAP, blocks, FF), bf16),
        input_output_aliases={10 + 2 * len(far): 0} if others else {},
        compiler_params=pltpu.CompilerParams(vmem_limit_bytes=60 * 1024 * 1024),
        cost_estimate=pl.CostEstimate(
            flops=3*10**9 if e == 0 else 2 * rows * D * 2 * FF,
            bytes_accessed=10_000_000,
            transcendentals=10**6,
        ),
    )(where, own, rest, own, rest, gates, sort, sort8, near, near, *far, *far, *others)


def over(axis, count, block):
    return [block] + [
        lax.ppermute(block, axis, [(i, (i + b) % count) for i in range(count)])
        for b in range(1, count)
    ]


def over_peers(message):
    return lax.all_to_all(message, ("y", "c"), split_axis=0, concat_axis=0, tiled=True)


def take_kernel(*refs):
    refs[-1][...] = refs[0][0]


def marks(*values):
    return [
        lax.slice(v, (0,) * v.ndim, (1,) * (v.ndim - 2) + (8, TOK)).reshape(8, TOK) for v in values
    ]


def take(weights, e, *others):
    shape = weights.shape[1:]
    others = marks(*others)
    return pl.pallas_call(
        take_kernel,
        grid=(1,),
        in_specs=[pl.BlockSpec((1,) + shape, lambda n: (e, 0, 0))]
        + [pl.BlockSpec(memory_space=pl.ANY)] * len(others),
        out_specs=pl.BlockSpec(shape, lambda n: (0, 0)),
        out_shape=jax.ShapeDtypeStruct(shape, weights.dtype),
        cost_estimate=pl.CostEstimate(flops=TAKE_COST[e], bytes_accessed=1_600_000, transcendentals=0),
    )(weights, *others)


def pass_kernel(*refs):
    pass


def after(value, *others):
    others = marks(*others)
    return pl.pallas_call(
        pass_kernel,
        in_specs=[pl.BlockSpec(memory_space=pl.ANY)] * (1 + len(others)),
        out_specs=pl.BlockSpec(memory_space=pl.ANY),
        out_shape=jax.ShapeDtypeStruct(value.shape, value.dtype),
        input_output_aliases={0: 0},
    )(value, *others)


def shards(moe_rows, expert_ids, expert_gates, expert_weights):
    zh, zl = lax.axis_index("zh"), lax.axis_index("zl")
    where = jnp.stack([zl, zh, lax.axis_index("x")])
    info = jnp.concatenate([expert_ids.T.astype(bf16), expert_gates.T], axis=1)
    packed = jnp.concatenate([moe_rows, jnp.pad(info, ((0, 0), (0, D - INFO)))], axis=0)
    blocks = over("zl", ZL, packed)
    near = lax.all_gather(expert_weights, "x", axis=0)
    own = over_peers(dispatch(zl.reshape(1), [packed]))
    swap = [(0, 1), (1, 0)]
    taken = take(expert_weights, 0, *blocks[1:])
    first = lax.ppermute(taken, "zh", swap)
    rest = over_peers(dispatch(zl.reshape(1), blocks, *marks(own, taken)))
    second = lax.ppermute(take(expert_weights, 1, first), "zh", swap)
    far = [over("x", X, first), over("x", X, second)]
    slots = plan(where, rest)
    hidden = expert(0, where, own, rest, slots, near, far[0])
    hidden = expert(1, where, own, rest, slots, near, far[1], hidden)
    return jnp.transpose(hidden, (0, 2, 1, 3))[None]


def solution(mesh):
    inner = Mesh(mesh.devices.reshape(ZH, X, ZL, Y, C), ("zh", "x", "zl", "y", "c"))
    tokens = P(("zh", "x", "zl", "y", "c"), None)
    in_specs = (tokens, tokens, tokens, P(("zl", "y", "c"), ("zh", "x"), None))
    out_specs = P(("zh", "x"), ("zl", "y", "c"), None, None, None)
    return jax.shard_map(
        shards, mesh=inner, in_specs=in_specs, out_specs=out_specs, check_vma=False
    )
```
